32 devices in a mesh: frame: 2 (over x), brick: 16 (over z, y, core).
Axes of the slice: x: 2, y: 2, z: 4, core: 2. Of those that a mesh axis runs over, the one named last changes fastest.
Arguments:
- intensity: float32 [8, 256, 128], P('frame', 'brick'), may hold values from 0.1 to 10
- correction: float32 [8, 256, 128], P('frame', 'brick'), may hold values from 0.3 to 3
- splitting: bfloat16 [8, 16, 8, 128, 512], P('frame', 'brick'), may hold values from 0 to 0.015625
- block_count: int32 [8, 16], P('frame', 'brick'), may hold values from 1 to 8, 64 in all within a row
- pix_index: int32 [8, 16, 8], P('frame', 'brick'), may hold values from 0 to 255, as said below
- vox_offset: int32 [8, 16, 8], P('frame', 'brick'), may hold values from 0 to 33
Outputs:
- merged: float32 [16, 32, 512], P('brick', 'frame')
- weight: float32 [16, 32, 512], P('brick', 'frame')
The draws below stay inside these ranges and needn't reach their ends.
Inputs may be any that keep to these rules, and one draw needn't show every extreme that they name: `block_count`: each frame's counts over the bricks sum to 64, and some pair of the frame holds 8. `pix_index`: the 32 slots of one device (its frames, its brick, padded slots included) include at most 4 slots (counted with repeats, over all of the device's frames) whose pixel block lies in the range 16 * c to 16 * c + 15, for every c; on every device some c has exactly 4 such slots.
All inputs are finite; a program needn't handle non-finite values. No bound on the sum of `block_count` on one device may be relied on, other than what follows from the above.
Results may differ from the reference program's by a relative error of at most 0.00049.
Values may be sent and summed in bfloat16 or wider, within the bound.
No kernel may reach another device: no remote copies, remote signals or barrier semaphores. Data moves between devices by JAX's collectives and lax.ppermute only.
A program may use at most 64 MiB of HBM per device.

```python
import math
import jax
import jax.numpy as jnp
import numpy as np
from jax import lax

P_SIZE = 128
V = 512
FR_DEV = 4
MAXB = 8
PB_DEV = 16
CAP = 4
FRAMES = 8
BRICKS = 16
PBLK = 256
BLK = 32


def draw_pix_index(key, part):
    frame_groups = FRAMES // FR_DEV
    slot_count = FR_DEV * MAXB
    subkeys = jax.random.split(key, frame_groups * BRICKS)

    def draw_device(device_key):
        key_top, key_pool, key_order, key_resident = jax.random.split(device_key, 4)
        top_owner = jax.random.randint(key_top, (), 0, BRICKS, dtype=jnp.int32)
        shuffled = jax.random.permutation(key_pool, (BRICKS - 1) * (CAP - 1))[:slot_count - CAP].astype(jnp.int32)
        others = shuffled // (CAP - 1)
        others = jnp.where(others >= top_owner, others + 1, others)
        owners = jnp.concatenate([jnp.full((CAP,), top_owner, dtype=jnp.int32), others])
        owners = jax.random.permutation(key_order, owners)
        local_block = jax.random.randint(key_resident, (slot_count,), 0, PB_DEV, dtype=jnp.int32)
        return owners * PB_DEV + local_block
    drawn = jax.vmap(draw_device)(subkeys)
    drawn = drawn.reshape(frame_groups, BRICKS, FR_DEV, MAXB)
    return jnp.transpose(drawn, (0, 2, 1, 3)).reshape(FRAMES, BRICKS, MAXB)


def plant(values, rng, low, top_value):
    extent = values.shape
    index_at = [jax.random.randint(jax.random.fold_in(rng, axis), (), 0, extent[axis]) for axis in range(len(extent))]
    values = values.at[tuple(index_at)].set(low)
    longest = extent.index(max(extent))
    index_at[longest] = (index_at[longest] + 1) % extent[longest]
    return values.at[tuple(index_at)].set(top_value)


def steps_of(rng, shape, pieces, low, largest):
    def one(dim, blocks):
        steps = jax.random.uniform(jax.random.fold_in(jax.random.fold_in(rng, 6), dim), (blocks,), jnp.float32, low / len(pieces), largest / len(pieces))
        return jnp.repeat(jnp.exp(steps), shape[dim] // blocks).reshape((-1,) + (1,) * (len(shape) - dim - 1))

    gain = one(*pieces[0])
    for cut in pieces[1:]:
        gain = gain * one(*cut)
    return gain


def profile(count, total, limit, skew):
    portions = [(1 << 20) // math.isqrt(rank ** skew) + 1 for rank in range(2, count + 1)]
    surplus, holding = total - limit - (count - 1), [1] * (count - 1)
    while surplus > 0:
        free = [i for i in range(count - 1) if holding[i] < limit]
        whole, remaining = sum([portions[i] for i in free]), surplus
        for i in free:
            extra = min(limit - holding[i], max(1, remaining * portions[i] // whole), surplus)
            holding[i] = holding[i] + extra
            surplus = surplus - extra
    return np.array([limit] + holding)


def uneven_parts(rng, count, total, limit, skew):
    if count == 2:
        one = jax.random.randint(rng, (), max(1, total - limit), min(limit, total - 1) + 1)
        return jnp.stack([one, total - one])
    lengths = jnp.asarray(profile(count, total, limit, skew), jnp.int32)
    pairs = (count - 1) // 2
    source_of, sink = lengths[1:1 + 2 * pairs:2], lengths[2:2 + 2 * pairs:2]
    room = jnp.minimum(source_of - 1, limit - sink)
    moved = jax.random.randint(jax.random.fold_in(rng, 1), (pairs,), 0, 1 << 20) % (room + 1)
    lengths = lengths.at[1:1 + 2 * pairs:2].set(source_of - moved).at[2:2 + 2 * pairs:2].set(sink + moved)
    return lengths[jax.random.permutation(jax.random.fold_in(rng, 2), count)]


def setup_inputs(seed: int = 0) -> dict:
    arg_keys = jax.random.split(jax.random.key(seed), 7)
    return {
        "intensity": jnp.clip(jnp.exp(math.log(10.0) - 4.6051702 * jax.random.uniform(arg_keys[0], (FRAMES, PBLK, P_SIZE), jnp.float32) ** steps_of(arg_keys[0], (FRAMES, PBLK, P_SIZE), ((0, 2), (1, 16)), -0.2, 0.2)), 0.1, 10.0),
        "correction": jnp.clip(jnp.exp(math.log(3.0) - 2.3025851 * jax.random.uniform(arg_keys[1], (FRAMES, PBLK, P_SIZE), jnp.float32) ** steps_of(arg_keys[1], (FRAMES, PBLK, P_SIZE), ((0, 2), (1, 16)), -0.2, 0.2)), 0.3, 3.0),
        "splitting": jnp.clip(0.015625 * jax.random.uniform(arg_keys[2], (FRAMES, BRICKS, MAXB, P_SIZE, V), jnp.float32) ** steps_of(arg_keys[2], (FRAMES, BRICKS, MAXB, P_SIZE, V), ((0, 2), (1, 16)), -0.2, 0.2), 0.0, 0.015625).astype(jnp.bfloat16),
        "block_count": jax.vmap(lambda own: uneven_parts(own, BRICKS, BRICKS * MAXB // 2, MAXB, 2))(jax.random.split(arg_keys[3], FRAMES)).reshape((FRAMES, BRICKS)).astype(jnp.int32),
        "pix_index": draw_pix_index(jax.random.fold_in(arg_keys[6], 71), 0),
        "vox_offset": plant(jax.random.randint(arg_keys[5], (FRAMES, BRICKS, MAXB), 0, BLK + 2), jax.random.fold_in(arg_keys[5], 1), 0, (BLK + 2) - 1).astype(jnp.int32),
    }


def reference(intensity, correction, splitting, block_count, pix_index, vox_offset):
    detector_pixel_rows = jnp.stack([intensity, correction], axis=2).astype(jnp.bfloat16)
    row_total = BRICKS * BLK
    brick_base = (jnp.arange(BRICKS, dtype=jnp.int32) * BLK)[:, None]
    slot_ids = jnp.arange(MAXB, dtype=jnp.int32)[None, :]

    def add_frame(totals, inputs):
        frame_rows, frame_split, counts, indices, offsets = inputs
        picked = frame_rows[indices]
        contrib = jnp.einsum("bmck,bmkv->bmcv", picked.astype(jnp.float32), frame_split.astype(jnp.float32), precision=lax.Precision.HIGHEST)
        target = brick_base + offsets - 1
        keep_mask = (slot_ids < counts[:, None]) & (target >= 0) & (target < row_total)
        contrib = jnp.where(keep_mask[:, :, None, None], contrib, jnp.float32(0.0))
        target = jnp.clip(target, 0, row_total - 1).astype(jnp.int32)
        totals = totals.at[target.reshape(-1)].add(contrib.reshape(BRICKS * MAXB, 2, V))
        return totals, jnp.float32(0.0)

    start = jnp.zeros((row_total, 2, V), jnp.float32)
    totals, unused = lax.scan(add_frame, start, (detector_pixel_rows, splitting, block_count, pix_index, vox_offset))
    weight = totals[:, 1].reshape(BRICKS, BLK, V)
    merged = totals[:, 0].reshape(BRICKS, BLK, V) / jnp.maximum(weight, 1.0)
    return merged, weight
```

```python
import functools

import jax
import jax.numpy as jnp
from jax import lax
from jax.experimental import pallas as pl
from jax.experimental.pallas import tpu as pltpu
from jax.sharding import PartitionSpec as P

BLK_DEV = 16
CHANNELS = 2
BLOCK_ROWS = CHANNELS * BLK_DEV + 8


def stages_of(bricks):
    if bricks == 16:
        return ((8,), (6, 2, 4), (1,))
    rounds, distance = [], bricks // 2
    while distance:
        rounds.append((distance,))
        distance //= 2
    return tuple(rounds)


def gather_rows(rows, bricks):
    held, distances = rows[None], [0]
    for exchange in stages_of(bricks):
        arrived = {
            step: lax.ppermute(held, "brick", [(i, i ^ step) for i in range(bricks)]) for step in exchange
        }
        order = sorted(arrived)
        held = jnp.concatenate([held] + [arrived[step] for step in order], axis=0)
        distances = distances + [d ^ step for step in order for d in distances]
    return held, distances


def place_of(distance, distances):
    place, bit = jnp.zeros_like(distance), 1
    while bit < len(distances):
        place = place + jnp.where((distance & bit) != 0, distances.index(bit), 0)
        bit *= 2
    return place


def split_kernel(frames, slots, groups, held_ref, meta_ref, split_ref, *refs):
    outs, placed_ref = refs[:groups], refs[groups]
    bricks, per_brick, pixels = held_ref.shape
    per_frame = per_brick // frames
    reach = bricks * per_frame
    pair = CHANNELS * slots
    sub = lax.broadcasted_iota(jnp.int32, (BLK_DEV, pixels), 0)
    lane = lax.broadcasted_iota(jnp.int32, (pair, pixels), 1)
    zero = jnp.zeros((BLK_DEV, pixels), jnp.float32)
    for frame in range(frames):
        target = meta_ref[pl.ds(frame * pair, pair), :]
        chosen = jnp.concatenate(
            [(target == lane + start).astype(jnp.float32) for start in range(0, reach, pixels)], axis=1
        ).astype(jnp.bfloat16)
        own = held_ref[:, pl.ds(frame * per_frame, per_frame), :].reshape(reach, pixels)
        picked = jnp.dot(chosen, own, preferred_element_type=jnp.float32)
        goal = meta_ref[pl.ds((frames + frame) * pair, pair), :]
        for slot in range(slots):
            first, second = CHANNELS * slot, CHANNELS * slot + 1
            value_0 = jnp.broadcast_to(picked[first : first + 1], sub.shape)
            value_1 = jnp.broadcast_to(picked[second : second + 1], sub.shape)
            goal_0 = jnp.broadcast_to(goal[first : first + 1], sub.shape)
            goal_1 = jnp.broadcast_to(goal[second : second + 1], sub.shape)
            parts = []
            for block in range(groups):
                base = block * BLOCK_ROWS
                parts.append(jnp.where(sub + base == goal_0, value_0, zero))
                parts.append(jnp.where(sub + (base + BLK_DEV) == goal_1, value_1, zero))
                edge = sub[:8] + (base + 2 * BLK_DEV)
                parts.append(
                    jnp.where(
                        edge == goal_0[:8], value_0[:8], jnp.where(edge == goal_1[:8], value_1[:8], zero[:8])
                    )
                )
            place = (frame * slots + slot) * pixels
            placed_ref[:, pl.ds(place, pixels)] = jnp.concatenate(parts, axis=0).astype(jnp.bfloat16)
    total = jnp.dot(placed_ref[...], split_ref[...], preferred_element_type=jnp.float32)
    for block in range(groups):
        outs[block][...] = total[block * BLOCK_ROWS : (block + 1) * BLOCK_ROWS]


def on_device(intensity, correction, splitting, block_count, pix_index, vox_offset):
    frames_dev, blocks_per_device, pixel_width = intensity.shape
    max_slots = splitting.shape[2]
    voxels = splitting.shape[4]
    bricks = lax.axis_size("brick")
    groups = lax.axis_size("frame")
    brick, group = lax.axis_index("brick"), lax.axis_index("frame")
    top = groups - 1
    block_rows = BLK_DEV * groups
    slot_count = frames_dev * max_slots

    local_rows = jnp.stack([intensity, correction], axis=2).astype(jnp.bfloat16)
    local_rows = local_rows.reshape(frames_dev * blocks_per_device * CHANNELS, pixel_width)
    held, distances = gather_rows(local_rows, bricks)

    channel = jnp.arange(CHANNELS, dtype=jnp.int32)
    indices = pix_index.reshape(slot_count)
    place = place_of((indices // blocks_per_device) ^ brick, distances)
    target = (place * blocks_per_device + indices % blocks_per_device)[:, None] * CHANNELS + channel
    offsets = vox_offset.reshape(slot_count)
    live = (jnp.arange(max_slots, dtype=jnp.int32)[None, :] < block_count).reshape(slot_count)
    low, high = offsets == 0, offsets == block_rows + 1
    live = live & ~(low & (brick == 0)) & ~(high & (brick == bricks - 1))
    owner = jnp.where(low, top, jnp.where(high, 0, (offsets - 1) // BLK_DEV))
    base = ((owner - group + groups) % groups) * BLOCK_ROWS
    inside = (offsets - 1) % BLK_DEV
    goal = jnp.where(
        (low | high)[:, None],
        CHANNELS * BLK_DEV + channel,
        inside[:, None] + BLK_DEV * channel,
    )
    goal = jnp.where(live[:, None], base[:, None] + goal, -1)
    meta = jnp.concatenate([target.reshape(-1), goal.reshape(-1)])
    meta = jnp.broadcast_to(meta[:, None], (2 * slot_count * CHANNELS, pixel_width))

    in_vmem = pl.BlockSpec(memory_space=pltpu.VMEM)
    blocks = pl.pallas_call(
        functools.partial(split_kernel, frames_dev, max_slots, groups),
        out_shape=[jax.ShapeDtypeStruct((BLOCK_ROWS, voxels), jnp.float32)] * groups,
        in_specs=[in_vmem] * 3,
        out_specs=[in_vmem] * groups,
        scratch_shapes=[pltpu.VMEM((groups * BLOCK_ROWS, slot_count * pixel_width), jnp.bfloat16)],
        compiler_params=pltpu.CompilerParams(vmem_limit_bytes=24 * 1024 * 1024),
        cost_estimate=pl.CostEstimate(
            flops=2 * groups * BLOCK_ROWS * slot_count * pixel_width * voxels,
            bytes_accessed=2 * slot_count * pixel_width * voxels,
            transcendentals=0,
        ),
        name="split_and_place",
    )(held, meta, splitting.reshape(slot_count * pixel_width, voxels))

    received = [
        lax.ppermute(blocks[step], "frame", [(i, (i + step) % groups) for i in range(groups)])
        for step in range(1, groups)
    ]
    edge = slice(CHANNELS * BLK_DEV, CHANNELS * BLK_DEV + CHANNELS)
    overhang = sum([part[edge] for part in received], blocks[0][edge])
    turn = [(i, i) for i in range(bricks, top * bricks)]
    for i in range(bricks):
        turn.append((i, i + 1 if i + 1 < bricks else top * bricks + i))
        turn.append((top * bricks + i, top * bricks + i - 1 if i else 0))
    handed = lax.ppermute(overhang, ("frame", "brick"), turn)
    interior = slice(0, CHANNELS * BLK_DEV)
    total = sum([part[interior] for part in received], blocks[0][interior])
    total = total.reshape(CHANNELS, BLK_DEV, voxels)
    row = jnp.where(group == 0, 0, jnp.where(group == top, BLK_DEV - 1, -1))
    here = jnp.arange(BLK_DEV, dtype=jnp.int32)[None, :, None] == row
    total = total + jnp.where(here, handed[:, None, :], 0.0)
    weight = total[1]
    merged = total[0] / jnp.maximum(weight, 1.0)
    return (merged[None], weight[None])


def solution(mesh):
    placed = (
        P("frame", "brick", None),
        P("frame", "brick", None),
        P("frame", "brick", None, None, None),
        P("frame", "brick"),
        P("frame", "brick", None),
        P("frame", "brick", None),
    )
    return jax.shard_map(
        on_device,
        mesh=mesh,
        in_specs=placed,
        out_specs=(P("brick", "frame", None), P("brick", "frame", None)),
        check_vma=False,
    )
```

```python
import functools

import jax
import jax.numpy as jnp
from jax import lax
from jax.experimental import pallas as pl
from jax.experimental.pallas import tpu as pltpu
from jax.sharding import PartitionSpec as P

BLK_DEV = 16
CHANNELS = 2
VMEM_LIMIT = 8 * 1024 * 1024
BLOCK_ROWS = CHANNELS * BLK_DEV + 8


def stages_of(bricks):
    if bricks == 16:
        return ((8,), (6, 2, 4), (1,))
    rounds, distance = [], bricks // 2
    while distance:
        rounds.append((distance,))
        distance //= 2
    return tuple(rounds)


def join_kernel(*refs):
    out_ref, at = refs[-1], 0
    for ref in refs[:-2]:
        out_ref[pl.ds(at, ref.shape[0])] = ref[...]
        at += ref.shape[0]


def join(parts, after):
    in_vmem = pl.BlockSpec(memory_space=pltpu.VMEM)
    count = sum(part.shape[0] for part in parts)
    return pl.pallas_call(
        join_kernel,
        out_shape=jax.ShapeDtypeStruct((count,) + parts[0].shape[1:], parts[0].dtype),
        in_specs=[in_vmem] * (len(parts) + 1),
        out_specs=in_vmem,
        compiler_params=pltpu.CompilerParams(vmem_limit_bytes=VMEM_LIMIT),
        name="join_rows",
    )(*parts, after)


def gather_rows(rows, bricks, beside):
    stages = stages_of(bricks)
    held, distances, made = rows[None], [0], None
    for exchange in stages:
        distances = distances + [d ^ step for step in sorted(exchange) for d in distances]
    for at, exchange in enumerate(stages):
        arrived = {
            step: lax.ppermute(held, "brick", [(i, i ^ step) for i in range(bricks)]) for step in exchange
        }
        parts = [held] + [arrived[step] for step in sorted(arrived)]
        if at == len(stages) - 2:
            made = beside(held, distances)
            held = join(parts, made)
        elif at < len(stages) - 1:
            held = jnp.concatenate(parts, axis=0)
    return parts, distances, made


def place_of(distance, distances):
    place, bit = 0, 1
    while bit < len(distances):
        place = place + jnp.where((distance & bit) != 0, distances.index(bit), 0)
        bit *= 2
    return place


def prepare_kernel(
    distances, per_owner, block_rows, bricks, groups, slots, index_ref, after_ref, split_ref, meta_ref
):
    brick, group = lax.axis_index("brick"), lax.axis_index("frame")
    frames = index_ref.shape[0] // 3
    wide = (slots * CHANNELS, meta_ref.shape[1])
    row = lax.broadcasted_iota(jnp.int32, wide, 0)
    channel = row % CHANNELS
    mine = lax.broadcasted_iota(jnp.int32, wide, 1) == row // CHANNELS

    def of_slot(at):
        line = jnp.broadcast_to(index_ref[pl.ds(at, 1), :], wide)
        return jnp.sum(jnp.where(mine, line, 0), axis=1, keepdims=True) + jnp.zeros(wide, jnp.int32)

    for frame in range(frames):
        pixel_block = of_slot(frame)
        owner = pixel_block // per_owner
        place = place_of(owner ^ brick, distances)
        target = (place * CHANNELS + channel) * per_owner + (pixel_block - owner * per_owner)
        meta_ref[pl.ds(frame * wide[0], wide[0]), :] = target
        offset = of_slot(frames + frame)
        low, high = offset == 0, offset == block_rows + 1
        holder = jnp.where(low, groups - 1, jnp.where(high, 0, (offset - 1) // BLK_DEV))
        step = holder - group
        step = jnp.where(step < 0, step + groups, step)
        inside = offset - 1 - holder * BLK_DEV + BLK_DEV * channel
        goal = step * BLOCK_ROWS + jnp.where(low | high, CHANNELS * BLK_DEV + channel, inside)
        live = row // CHANNELS < of_slot(2 * frames + frame)
        live = live & ~(low & (brick == 0)) & ~(high & (brick == bricks - 1))
        meta_ref[pl.ds((frames + frame) * wide[0], wide[0]), :] = jnp.where(live, goal, -1)


def split_kernel(frames, slots, groups, near_ref, far_ref, meta_ref, split_ref, *refs):
    outs, placed_ref = refs[:groups], refs[groups]
    half, per_brick, pixels = near_ref.shape
    per_owner = per_brick // (CHANNELS * frames)
    reach = 2 * half * CHANNELS * per_owner
    pair = CHANNELS * slots
    sub = lax.broadcasted_iota(jnp.int32, (BLK_DEV, pixels), 0)
    lane = lax.broadcasted_iota(jnp.int32, (pair, pixels), 1)
    zero = jnp.zeros((BLK_DEV, pixels), jnp.float32)
    for frame in range(frames):
        target = meta_ref[pl.ds(frame * pair, pair), :]
        chosen = jnp.concatenate(
            [(target == lane + start).astype(jnp.float32) for start in range(0, reach, pixels)], axis=1
        ).astype(jnp.bfloat16)
        own = jnp.concatenate(
            [
                jnp.concatenate(
                    [ref[:, pl.ds((c * frames + frame) * per_owner, per_owner), :] for c in range(CHANNELS)],
                    axis=1,
                ).reshape(reach // 2, pixels)
                for ref in (near_ref, far_ref)
            ],
            axis=0,
        )
        picked = jnp.dot(chosen, own, preferred_element_type=jnp.float32)
        goal = meta_ref[pl.ds((frames + frame) * pair, pair), :]
        for slot in range(slots):
            first, second = CHANNELS * slot, CHANNELS * slot + 1
            value_0 = jnp.broadcast_to(picked[first : first + 1], sub.shape)
            value_1 = jnp.broadcast_to(picked[second : second + 1], sub.shape)
            goal_0 = jnp.broadcast_to(goal[first : first + 1], sub.shape)
            goal_1 = jnp.broadcast_to(goal[second : second + 1], sub.shape)
            parts = []
            for block in range(groups):
                base = block * BLOCK_ROWS
                parts.append(jnp.where(sub + base == goal_0, value_0, zero))
                parts.append(jnp.where(sub + (base + BLK_DEV) == goal_1, value_1, zero))
                edge = sub[:8] + (base + 2 * BLK_DEV)
                parts.append(
                    jnp.where(
                        edge == goal_0[:8], value_0[:8], jnp.where(edge == goal_1[:8], value_1[:8], zero[:8])
                    )
                )
            place = (frame * slots + slot) * pixels
            placed_ref[:, pl.ds(place, pixels)] = jnp.concatenate(parts, axis=0).astype(jnp.bfloat16)
    total = jnp.dot(placed_ref[...], split_ref[...], preferred_element_type=jnp.float32)
    for block in range(groups):
        outs[block][...] = total[block * BLOCK_ROWS : (block + 1) * BLOCK_ROWS]


def finish_kernel(groups, handed_ref, *refs):
    parts, (merged_ref, weight_ref) = refs[:groups], refs[groups:]
    group = lax.axis_index("frame")
    row = jnp.where(group == 0, 0, jnp.where(group == groups - 1, BLK_DEV - 1, -1))
    here = lax.broadcasted_iota(jnp.int32, merged_ref.shape, 0) == row
    totals = []
    for c in range(CHANNELS):
        rows = pl.ds(c * BLK_DEV, BLK_DEV)
        total = jnp.where(here, handed_ref[pl.ds(c, 1), :], 0.0)
        for part in parts:
            total = total + part[rows, :]
        totals.append(total)
    weight_ref[...] = totals[1]
    merged_ref[...] = totals[0] / jnp.maximum(totals[1], 1.0)


def on_device(intensity, correction, splitting, block_count, pix_index, vox_offset):
    frames_dev, blocks_per_device, pixel_width = intensity.shape
    max_slots = splitting.shape[2]
    voxels = splitting.shape[4]
    bricks = lax.axis_size("brick")
    groups = lax.axis_size("frame")
    top = groups - 1
    block_rows = BLK_DEV * groups
    slot_count = frames_dev * max_slots

    in_vmem = pl.BlockSpec(memory_space=pltpu.VMEM)
    row_count = frames_dev * blocks_per_device
    local_rows = jnp.stack([intensity, correction], axis=0).astype(jnp.bfloat16)
    local_rows = local_rows.reshape(CHANNELS * row_count, pixel_width)
    depth = slot_count * pixel_width

    counts = jnp.broadcast_to(block_count, (frames_dev, max_slots))
    indices = [pix_index.reshape(frames_dev, max_slots), vox_offset.reshape(frames_dev, max_slots), counts]
    indices = jnp.pad(jnp.concatenate(indices, axis=0), ((0, 0), (0, pixel_width - max_slots)))
    split = splitting.reshape(depth, voxels)

    def prepare(first, distances):
        return pl.pallas_call(
            functools.partial(
                prepare_kernel, distances, blocks_per_device, block_rows, bricks, groups, max_slots
            ),
            out_shape=jax.ShapeDtypeStruct((2 * CHANNELS * slot_count, pixel_width), jnp.int32),
            in_specs=[in_vmem] * 3,
            out_specs=in_vmem,
            compiler_params=pltpu.CompilerParams(vmem_limit_bytes=VMEM_LIMIT),
            cost_estimate=pl.CostEstimate(flops=0, bytes_accessed=4 * depth * voxels, transcendentals=0),
            name="prepare",
        )(indices, first, split)

    (near, far), distances, meta = gather_rows(local_rows, bricks, prepare)
    blocks = pl.pallas_call(
        functools.partial(split_kernel, frames_dev, max_slots, groups),
        out_shape=[jax.ShapeDtypeStruct((BLOCK_ROWS, voxels), jnp.float32)] * groups,
        in_specs=[in_vmem] * 4,
        out_specs=[in_vmem] * groups,
        scratch_shapes=[pltpu.VMEM((groups * BLOCK_ROWS, slot_count * pixel_width), jnp.bfloat16)],
        compiler_params=pltpu.CompilerParams(vmem_limit_bytes=VMEM_LIMIT),
        cost_estimate=pl.CostEstimate(
            flops=2 * groups * BLOCK_ROWS * slot_count * pixel_width * voxels,
            bytes_accessed=2 * slot_count * pixel_width * voxels,
            transcendentals=0,
        ),
        name="split_and_place",
    )(near, far, meta, split)

    received = [
        lax.ppermute(blocks[step], "frame", [(i, (i + step) % groups) for i in range(groups)])
        for step in range(1, groups)
    ]
    edge = slice(CHANNELS * BLK_DEV, CHANNELS * BLK_DEV + CHANNELS)
    overhang = sum([part[edge] for part in received], blocks[0][edge])
    turn = [(i, i) for i in range(bricks, top * bricks)]
    for i in range(bricks):
        turn.append((i, i + 1 if i + 1 < bricks else top * bricks + i))
        turn.append((top * bricks + i, top * bricks + i - 1 if i else 0))
    handed = lax.ppermute(overhang, ("frame", "brick"), turn)
    merged, weight = pl.pallas_call(
        functools.partial(finish_kernel, groups),
        out_shape=[jax.ShapeDtypeStruct((BLK_DEV, voxels), jnp.float32)] * 2,
        in_specs=[in_vmem] * (groups + 1),
        out_specs=[in_vmem] * 2,
        compiler_params=pltpu.CompilerParams(vmem_limit_bytes=VMEM_LIMIT),
        name="finish",
    )(handed, blocks[0], *received)
    return (merged[None], weight[None])


def solution(mesh):
    placed = (
        P("frame", "brick", None),
        P("frame", "brick", None),
        P("frame", "brick", None, None, None),
        P("frame", "brick"),
        P("frame", "brick", None),
        P("frame", "brick", None),
    )
    return jax.shard_map(
        on_device,
        mesh=mesh,
        in_specs=placed,
        out_specs=(P("brick", "frame", None), P("brick", "frame", None)),
        check_vma=False,
    )
```

```python
import functools

import jax
import jax.numpy as jnp
from jax import lax
from jax.experimental import pallas as pl
from jax.experimental.pallas import tpu as pltpu
from jax.sharding import PartitionSpec as P

BLK_DEV = 16
CHANNELS = 2
VMEM_LIMIT = 8 * 1024 * 1024
BLOCK_ROWS = CHANNELS * BLK_DEV + 8


def stages_of(bricks):
    if bricks == 16:
        return ((8,), (6, 2, 4), (1,))
    rounds, distance = [], bricks // 2
    while distance:
        rounds.append((distance,))
        distance //= 2
    return tuple(rounds)


def join_kernel(*refs):
    out_ref, at = refs[-1], 0
    for ref in refs[:-2]:
        out_ref[pl.ds(at, ref.shape[0])] = ref[...]
        at += ref.shape[0]


def join(parts, after):
    in_vmem = pl.BlockSpec(memory_space=pltpu.VMEM)
    count = sum(part.shape[0] for part in parts)
    return pl.pallas_call(
        join_kernel,
        out_shape=jax.ShapeDtypeStruct((count,) + parts[0].shape[1:], parts[0].dtype),
        in_specs=[in_vmem] * (len(parts) + 1),
        out_specs=in_vmem,
        compiler_params=pltpu.CompilerParams(vmem_limit_bytes=VMEM_LIMIT),
        name="join_rows",
    )(*parts, after)


def gather_rows(rows, bricks, beside):
    stages = stages_of(bricks)
    held, distances, made = rows[None], [0], None
    for exchange in stages:
        distances = distances + [d ^ step for step in sorted(exchange) for d in distances]
    for at, exchange in enumerate(stages):
        arrived = {
            step: lax.ppermute(held, "brick", [(i, i ^ step) for i in range(bricks)]) for step in exchange
        }
        parts = [held] + [arrived[step] for step in sorted(arrived)]
        if at == len(stages) - 2:
            made = beside(held, distances)
            held = join(parts, made)
        elif at < len(stages) - 1:
            held = jnp.concatenate(parts, axis=0)
    return parts, distances, made


def place_of(distance, distances):
    place, bit = 0, 1
    while bit < len(distances):
        place = place + jnp.where((distance & bit) != 0, distances.index(bit), 0)
        bit *= 2
    return place


def prepare_kernel(
    distances, per_owner, block_rows, bricks, groups, slots, index_ref, after_ref, split_ref, meta_ref
):
    brick, group = lax.axis_index("brick"), lax.axis_index("frame")
    frames = index_ref.shape[0] // 3
    wide = (slots * CHANNELS, meta_ref.shape[1])
    row = lax.broadcasted_iota(jnp.int32, wide, 0)
    channel = row % CHANNELS
    mine = lax.broadcasted_iota(jnp.int32, wide, 1) == row // CHANNELS

    def of_slot(at):
        line = jnp.broadcast_to(index_ref[pl.ds(at, 1), :], wide)
        return jnp.sum(jnp.where(mine, line, 0), axis=1, keepdims=True) + jnp.zeros(wide, jnp.int32)

    for frame in range(frames):
        pixel_block = of_slot(frame)
        owner = pixel_block // per_owner
        place = place_of(owner ^ brick, distances)
        target = (place * CHANNELS + channel) * per_owner + (pixel_block - owner * per_owner)
        meta_ref[pl.ds(frame * wide[0], wide[0]), :] = target
        offset = of_slot(frames + frame)
        low, high = offset == 0, offset == block_rows + 1
        holder = jnp.where(low, groups - 1, jnp.where(high, 0, (offset - 1) // BLK_DEV))
        step = holder - group
        step = jnp.where(step < 0, step + groups, step)
        inside = offset - 1 - holder * BLK_DEV + BLK_DEV * channel
        goal = step * BLOCK_ROWS + jnp.where(low | high, CHANNELS * BLK_DEV + channel, inside)
        live = row // CHANNELS < of_slot(2 * frames + frame)
        live = live & ~(low & (brick == 0)) & ~(high & (brick == bricks - 1))
        meta_ref[pl.ds((frames + frame) * wide[0], wide[0]), :] = jnp.where(live, goal, -1)


def edge_kernel(frames, slots, groups, near_ref, far_ref, meta_ref, split_ref, *refs):
    picked_ref, edges, placed_ref = refs[0], refs[1 : 1 + groups], refs[1 + groups]
    half, per_brick, pixels = near_ref.shape
    per_owner = per_brick // (CHANNELS * frames)
    reach = 2 * half * CHANNELS * per_owner
    pair = CHANNELS * slots
    lane = lax.broadcasted_iota(jnp.int32, (pair, pixels), 1)
    row = lax.broadcasted_iota(jnp.int32, (placed_ref.shape[0], pixels), 0)
    row = row // CHANNELS * BLOCK_ROWS + CHANNELS * BLK_DEV + row % CHANNELS
    for frame in range(frames):
        target = meta_ref[pl.ds(frame * pair, pair), :]
        chosen = jnp.concatenate(
            [(target == lane + start).astype(jnp.float32) for start in range(0, reach, pixels)], axis=1
        ).astype(jnp.bfloat16)
        own = jnp.concatenate(
            [
                jnp.concatenate(
                    [ref[:, pl.ds((c * frames + frame) * per_owner, per_owner), :] for c in range(CHANNELS)],
                    axis=1,
                ).reshape(reach // 2, pixels)
                for ref in (near_ref, far_ref)
            ],
            axis=0,
        )
        picked = jnp.dot(chosen, own, preferred_element_type=jnp.float32)
        picked_ref[pl.ds(frame * pair, pair), :] = picked
        goal = meta_ref[pl.ds((frames + frame) * pair, pair), :]
        for slot in range(slots):
            laid = jnp.zeros(row.shape, jnp.float32)
            for c in range(CHANNELS):
                at = CHANNELS * slot + c
                value = jnp.broadcast_to(picked[at : at + 1], row.shape)
                laid = jnp.where(row == jnp.broadcast_to(goal[at : at + 1], row.shape), value, laid)
            place = (frame * slots + slot) * pixels
            placed_ref[:, pl.ds(place, pixels)] = laid.astype(jnp.bfloat16)
    total = jnp.dot(placed_ref[...], split_ref[...], preferred_element_type=jnp.float32)
    for block in range(groups):
        edges[block][...] = total[CHANNELS * block : CHANNELS * (block + 1)]


def inner_kernel(frames, slots, groups, picked_ref, meta_ref, split_ref, *refs):
    inner, placed_ref = refs[:groups], refs[groups]
    pixels = picked_ref.shape[1]
    pair = CHANNELS * slots
    row = lax.broadcasted_iota(jnp.int32, (BLK_DEV, pixels), 0)
    zero = jnp.zeros(row.shape, jnp.float32)
    for frame in range(frames):
        picked = picked_ref[pl.ds(frame * pair, pair), :]
        goal = meta_ref[pl.ds((frames + frame) * pair, pair), :]
        for slot in range(slots):
            parts = []
            for block in range(groups):
                for c in range(CHANNELS):
                    at = CHANNELS * slot + c
                    value = jnp.broadcast_to(picked[at : at + 1], row.shape)
                    here = jnp.broadcast_to(goal[at : at + 1], row.shape) - (block * BLOCK_ROWS + c * BLK_DEV)
                    parts.append(jnp.where(row == here, value, zero))
            place = (frame * slots + slot) * pixels
            placed_ref[:, pl.ds(place, pixels)] = jnp.concatenate(parts, axis=0).astype(jnp.bfloat16)
    total = jnp.dot(placed_ref[...], split_ref[...], preferred_element_type=jnp.float32)
    for block in range(groups):
        base = block * CHANNELS * BLK_DEV
        inner[block][...] = total[base : base + CHANNELS * BLK_DEV]


def sum_kernel(*refs):
    total = refs[0][...]
    for ref in refs[1:-1]:
        total = total + ref[...]
    refs[-1][...] = total


def finish_kernel(groups, handed_ref, *refs):
    parts, (merged_ref, weight_ref) = refs[:groups], refs[groups:]
    group = lax.axis_index("frame")
    row = jnp.where(group == 0, 0, jnp.where(group == groups - 1, BLK_DEV - 1, -1))
    here = lax.broadcasted_iota(jnp.int32, merged_ref.shape, 0) == row
    totals = []
    for c in range(CHANNELS):
        rows = pl.ds(c * BLK_DEV, BLK_DEV)
        total = jnp.where(here, handed_ref[pl.ds(c, 1), :], 0.0)
        for part in parts:
            total = total + part[rows, :]
        totals.append(total)
    weight_ref[...] = totals[1]
    merged_ref[...] = totals[0] / jnp.maximum(totals[1], 1.0)


def on_device(intensity, correction, splitting, block_count, pix_index, vox_offset):
    frames_dev, blocks_per_device, pixel_width = intensity.shape
    max_slots = splitting.shape[2]
    voxels = splitting.shape[4]
    bricks = lax.axis_size("brick")
    groups = lax.axis_size("frame")
    top = groups - 1
    block_rows = BLK_DEV * groups
    slot_count = frames_dev * max_slots

    in_vmem = pl.BlockSpec(memory_space=pltpu.VMEM)
    row_count = frames_dev * blocks_per_device
    local_rows = jnp.stack([intensity, correction], axis=0).astype(jnp.bfloat16)
    local_rows = local_rows.reshape(CHANNELS * row_count, pixel_width)
    depth = slot_count * pixel_width

    counts = jnp.broadcast_to(block_count, (frames_dev, max_slots))
    indices = [pix_index.reshape(frames_dev, max_slots), vox_offset.reshape(frames_dev, max_slots), counts]
    indices = jnp.pad(jnp.concatenate(indices, axis=0), ((0, 0), (0, pixel_width - max_slots)))
    split = splitting.reshape(depth, voxels)

    def prepare(first, distances):
        return pl.pallas_call(
            functools.partial(
                prepare_kernel, distances, blocks_per_device, block_rows, bricks, groups, max_slots
            ),
            out_shape=jax.ShapeDtypeStruct((2 * CHANNELS * slot_count, pixel_width), jnp.int32),
            in_specs=[in_vmem] * 3,
            out_specs=in_vmem,
            compiler_params=pltpu.CompilerParams(vmem_limit_bytes=VMEM_LIMIT),
            cost_estimate=pl.CostEstimate(flops=0, bytes_accessed=4 * depth * voxels, transcendentals=0),
            name="prepare",
        )(indices, first, split)

    (near, far), distances, meta = gather_rows(local_rows, bricks, prepare)
    edge_rows = -(-CHANNELS * groups // 16) * 16
    inner_rows = CHANNELS * BLK_DEV * groups
    picked, *edges = pl.pallas_call(
        functools.partial(edge_kernel, frames_dev, max_slots, groups),
        out_shape=[jax.ShapeDtypeStruct((CHANNELS * slot_count, pixel_width), jnp.float32)]
        + [jax.ShapeDtypeStruct((CHANNELS, voxels), jnp.float32)] * groups,
        in_specs=[in_vmem] * 4,
        out_specs=[in_vmem] * (1 + groups),
        scratch_shapes=[pltpu.VMEM((edge_rows, depth), jnp.bfloat16)],
        compiler_params=pltpu.CompilerParams(vmem_limit_bytes=VMEM_LIMIT),
        cost_estimate=pl.CostEstimate(
            flops=2 * edge_rows * depth * voxels, bytes_accessed=2 * depth * voxels, transcendentals=0
        ),
        name="edges",
    )(near, far, meta, split)
    blocks = pl.pallas_call(
        functools.partial(inner_kernel, frames_dev, max_slots, groups),
        out_shape=[jax.ShapeDtypeStruct((CHANNELS * BLK_DEV, voxels), jnp.float32)] * groups,
        in_specs=[in_vmem] * 3,
        out_specs=[in_vmem] * groups,
        scratch_shapes=[pltpu.VMEM((inner_rows, depth), jnp.bfloat16)],
        compiler_params=pltpu.CompilerParams(vmem_limit_bytes=VMEM_LIMIT),
        cost_estimate=pl.CostEstimate(
            flops=2 * inner_rows * depth * voxels, bytes_accessed=2 * depth * voxels, transcendentals=0
        ),
        name="inner",
    )(picked, meta, split)

    def to_owner(parts):
        return [
            lax.ppermute(parts[step], "frame", [(i, (i + step) % groups) for i in range(groups)])
            for step in range(1, groups)
        ]

    arrived = to_owner(edges)
    overhang = pl.pallas_call(
        sum_kernel,
        out_shape=jax.ShapeDtypeStruct((CHANNELS, voxels), jnp.float32),
        in_specs=[in_vmem] * groups,
        out_specs=in_vmem,
        compiler_params=pltpu.CompilerParams(vmem_limit_bytes=VMEM_LIMIT),
        cost_estimate=pl.CostEstimate(flops=10**9, bytes_accessed=0, transcendentals=0),
        name="sum_edges",
    )(edges[0], *arrived)
    received = to_owner(blocks)
    turn = [(i, i) for i in range(bricks, top * bricks)]
    for i in range(bricks):
        turn.append((i, i + 1 if i + 1 < bricks else top * bricks + i))
        turn.append((top * bricks + i, top * bricks + i - 1 if i else 0))
    handed = lax.ppermute(overhang, ("frame", "brick"), turn)
    merged, weight = pl.pallas_call(
        functools.partial(finish_kernel, groups),
        out_shape=[jax.ShapeDtypeStruct((BLK_DEV, voxels), jnp.float32)] * 2,
        in_specs=[in_vmem] * (groups + 1),
        out_specs=[in_vmem] * 2,
        compiler_params=pltpu.CompilerParams(vmem_limit_bytes=VMEM_LIMIT),
        name="finish",
    )(handed, blocks[0], *received)
    return (merged[None], weight[None])


def solution(mesh):
    placed = (
        P("frame", "brick", None),
        P("frame", "brick", None),
        P("frame", "brick", None, None, None),
        P("frame", "brick"),
        P("frame", "brick", None),
        P("frame", "brick", None),
    )
    return jax.shard_map(
        on_device,
        mesh=mesh,
        in_specs=placed,
        out_specs=(P("brick", "frame", None), P("brick", "frame", None)),
        check_vma=False,
    )
```

```python
import functools

import jax
import jax.numpy as jnp
from jax import lax
from jax.experimental import pallas as pl
from jax.experimental.pallas import tpu as pltpu
from jax.sharding import PartitionSpec as P

BLK_DEV = 16
CHANNELS = 2
VMEM_LIMIT = 8 * 1024 * 1024
BLOCK_ROWS = CHANNELS * BLK_DEV + 8


def join_kernel(*refs):
    out_ref, at = refs[-1], 0
    for ref in refs[:-1]:
        out_ref[pl.ds(at, ref.shape[0])] = ref[...]
        at += ref.shape[0]


def join(parts):
    in_vmem = pl.BlockSpec(memory_space=pltpu.VMEM)
    count = sum(part.shape[0] for part in parts)
    return pl.pallas_call(
        join_kernel,
        out_shape=jax.ShapeDtypeStruct((count,) + parts[0].shape[1:], parts[0].dtype),
        in_specs=[in_vmem] * len(parts),
        out_specs=in_vmem,
        compiler_params=pltpu.CompilerParams(vmem_limit_bytes=VMEM_LIMIT),
        cost_estimate=pl.CostEstimate(flops=10**11, bytes_accessed=0, transcendentals=0),
        name="join_rows",
    )(*parts)


def swap(rows, bricks, step):
    return lax.ppermute(rows, "brick", [(i, i ^ step) for i in range(bricks)])


def gather_half(rows, bricks):
    held, distances = rows[None], [0]
    if bricks == 16:
        parts = [held, swap(held, bricks, 8), swap(held, bricks, 2)]
        corner = swap(held, bricks, 14)
        three = jnp.concatenate(parts, axis=0)
        parts = [join([three]), swap(three, bricks, 4), swap(parts[1], bricks, 2), corner]
        distances = [0, 8, 2, 4, 12, 6, 10, 14]
    else:
        parts, step = [held], bricks // 2
        while step > 1:
            arrived = swap(jnp.concatenate(parts, axis=0), bricks, step)
            parts, distances = parts + [arrived], distances + [d ^ step for d in distances]
            step //= 2
    return join(parts), distances + [d ^ 1 for d in distances]


def place_of(distance, distances):
    place = 0
    for at, d in enumerate(distances):
        place = place + jnp.where(distance == d, at, 0)
    return place


def prepare_kernel(distances, per_owner, block_rows, bricks, groups, slots, index_ref, meta_ref):
    brick, group = lax.axis_index("brick"), lax.axis_index("frame")
    frames = index_ref.shape[0]
    pair = slots * CHANNELS
    wide = (pair, meta_ref.shape[1])
    row = lax.broadcasted_iota(jnp.int32, wide, 0)
    channel = row % CHANNELS
    mine = lax.broadcasted_iota(jnp.int32, (pair, slots), 1) == (
        lax.broadcasted_iota(jnp.int32, (pair, slots), 0) // CHANNELS
    )
    for frame in range(frames):
        line = jnp.broadcast_to(index_ref[pl.ds(frame, 1), :], mine.shape)
        index = jnp.broadcast_to(jnp.sum(jnp.where(mine, line, 0), axis=1, keepdims=True), wide)
        pixel_block = index // (block_rows + 3)
        offset = index - pixel_block * (block_rows + 3)
        owner = pixel_block // per_owner
        place = place_of(owner ^ brick, distances)
        target = (place * CHANNELS + channel) * per_owner + (pixel_block - owner * per_owner)
        meta_ref[pl.ds(frame * pair, pair), :] = target
        low, high = offset == 0, offset == block_rows + 1
        holder = jnp.where(low, groups - 1, jnp.where(high, 0, (offset - 1) // BLK_DEV))
        step = holder - group
        step = jnp.where(step < 0, step + groups, step)
        inside = offset - 1 - holder * BLK_DEV + BLK_DEV * channel
        goal = step * BLOCK_ROWS + jnp.where(low | high, CHANNELS * BLK_DEV + channel, inside)
        live = offset < block_rows + 2
        live = live & ~(low & (brick == 0)) & ~(high & (brick == bricks - 1))
        meta_ref[pl.ds((frames + frame) * pair, pair), :] = jnp.where(live, goal, -1)


def edge_kernel(frames, slots, groups, near_ref, far_ref, meta_ref, split_ref, *refs):
    picked_ref, edges, placed_ref = refs[0], refs[1 : 1 + groups], refs[1 + groups]
    half, per_brick, pixels = near_ref.shape
    per_owner = per_brick // (CHANNELS * frames)
    reach = 2 * half * CHANNELS * per_owner
    pair = CHANNELS * slots
    lane = lax.broadcasted_iota(jnp.int32, (pair, pixels), 1)
    row = lax.broadcasted_iota(jnp.int32, (placed_ref.shape[0], pixels), 0)
    row = row // CHANNELS * BLOCK_ROWS + CHANNELS * BLK_DEV + row % CHANNELS
    for frame in range(frames):
        target = meta_ref[pl.ds(frame * pair, pair), :]
        chosen = jnp.concatenate(
            [(target == lane + start).astype(jnp.float32) for start in range(0, reach, pixels)], axis=1
        ).astype(jnp.bfloat16)
        own = jnp.concatenate(
            [
                jnp.concatenate(
                    [ref[:, pl.ds((c * frames + frame) * per_owner, per_owner), :] for c in range(CHANNELS)],
                    axis=1,
                ).reshape(reach // 2, pixels)
                for ref in (near_ref, far_ref)
            ],
            axis=0,
        )
        picked = jnp.dot(chosen, own, preferred_element_type=jnp.float32)
        picked_ref[pl.ds(frame * pair, pair), :] = picked
        goal = meta_ref[pl.ds((frames + frame) * pair, pair), :]
        for slot in range(slots):
            laid = jnp.zeros(row.shape, jnp.float32)
            for c in range(CHANNELS):
                at = CHANNELS * slot + c
                value = jnp.broadcast_to(picked[at : at + 1], row.shape)
                laid = jnp.where(row == jnp.broadcast_to(goal[at : at + 1], row.shape), value, laid)
            place = (frame * slots + slot) * pixels
            placed_ref[:, pl.ds(place, pixels)] = laid.astype(jnp.bfloat16)
    total = jnp.dot(placed_ref[...], split_ref[...], preferred_element_type=jnp.float32)
    for block in range(groups):
        edges[block][...] = total[CHANNELS * block : CHANNELS * (block + 1)]


def inner_kernel(frames, slots, groups, picked_ref, meta_ref, split_ref, *refs):
    inner, placed_ref = refs[:groups], refs[groups]
    pixels = picked_ref.shape[1]
    pair = CHANNELS * slots
    row = lax.broadcasted_iota(jnp.int32, (BLK_DEV, pixels), 0)
    zero = jnp.zeros(row.shape, jnp.float32)
    for frame in range(frames):
        picked = picked_ref[pl.ds(frame * pair, pair), :]
        goal = meta_ref[pl.ds((frames + frame) * pair, pair), :]
        for slot in range(slots):
            parts = []
            for block in range(groups):
                for c in range(CHANNELS):
                    at = CHANNELS * slot + c
                    value = jnp.broadcast_to(picked[at : at + 1], row.shape)
                    here = jnp.broadcast_to(goal[at : at + 1], row.shape) - (block * BLOCK_ROWS + c * BLK_DEV)
                    parts.append(jnp.where(row == here, value, zero))
            place = (frame * slots + slot) * pixels
            placed_ref[:, pl.ds(place, pixels)] = jnp.concatenate(parts, axis=0).astype(jnp.bfloat16)
    total = jnp.dot(placed_ref[...], split_ref[...], preferred_element_type=jnp.float32)
    for block in range(groups):
        base = block * CHANNELS * BLK_DEV
        inner[block][...] = total[base : base + CHANNELS * BLK_DEV]


def sum_kernel(*refs):
    total = refs[0][...]
    for ref in refs[1:-1]:
        total = total + ref[...]
    refs[-1][...] = total


def finish_kernel(groups, handed_ref, *refs):
    parts, (merged_ref, weight_ref) = refs[:groups], refs[groups:]
    group = lax.axis_index("frame")
    row = jnp.where(group == 0, 0, jnp.where(group == groups - 1, BLK_DEV - 1, -1))
    here = lax.broadcasted_iota(jnp.int32, merged_ref.shape, 0) == row
    totals = []
    for c in range(CHANNELS):
        rows = pl.ds(c * BLK_DEV, BLK_DEV)
        total = jnp.where(here, handed_ref[pl.ds(c, 1), :], 0.0)
        for part in parts:
            total = total + part[rows, :]
        totals.append(total)
    weight_ref[...] = totals[1]
    merged_ref[...] = totals[0] / jnp.maximum(totals[1], 1.0)


def on_device(intensity, correction, splitting, block_count, pix_index, vox_offset):
    frames_dev, blocks_per_device, pixel_width = intensity.shape
    max_slots = splitting.shape[2]
    voxels = splitting.shape[4]
    bricks = lax.axis_size("brick")
    groups = lax.axis_size("frame")
    top = groups - 1
    block_rows = BLK_DEV * groups
    slot_count = frames_dev * max_slots

    in_vmem = pl.BlockSpec(memory_space=pltpu.VMEM)
    row_count = frames_dev * blocks_per_device
    local_rows = jnp.stack([intensity, correction], axis=0).astype(jnp.bfloat16)
    local_rows = local_rows.reshape(CHANNELS * row_count, pixel_width)
    depth = slot_count * pixel_width

    split = splitting.reshape(depth, voxels)

    near, distances = gather_half(local_rows, bricks)
    near, block_count, pix_index, vox_offset = lax.optimization_barrier(
        (near, block_count, pix_index, vox_offset)
    )
    far = swap(near, bricks, 1)
    live = jnp.arange(max_slots, dtype=jnp.int32) < block_count[:, :, None]
    index = pix_index * (block_rows + 3) + jnp.where(live, vox_offset, block_rows + 2)
    meta = pl.pallas_call(
        functools.partial(
            prepare_kernel, distances, blocks_per_device, block_rows, bricks, groups, max_slots
        ),
        out_shape=jax.ShapeDtypeStruct((2 * CHANNELS * slot_count, pixel_width), jnp.int32),
        in_specs=[in_vmem],
        out_specs=in_vmem,
        compiler_params=pltpu.CompilerParams(vmem_limit_bytes=VMEM_LIMIT),
        name="prepare",
    )(index.reshape(frames_dev, max_slots))

    edge_rows = -(-CHANNELS * groups // 16) * 16
    inner_rows = CHANNELS * BLK_DEV * groups
    picked, *edges = pl.pallas_call(
        functools.partial(edge_kernel, frames_dev, max_slots, groups),
        out_shape=[jax.ShapeDtypeStruct((CHANNELS * slot_count, pixel_width), jnp.float32)]
        + [jax.ShapeDtypeStruct((CHANNELS, voxels), jnp.float32)] * groups,
        in_specs=[in_vmem] * 4,
        out_specs=[in_vmem] * (1 + groups),
        scratch_shapes=[pltpu.VMEM((edge_rows, depth), jnp.bfloat16)],
        compiler_params=pltpu.CompilerParams(vmem_limit_bytes=VMEM_LIMIT),
        cost_estimate=pl.CostEstimate(
            flops=2 * edge_rows * depth * voxels, bytes_accessed=2 * depth * voxels, transcendentals=0
        ),
        name="edges",
    )(near, far, meta, split)
    blocks = pl.pallas_call(
        functools.partial(inner_kernel, frames_dev, max_slots, groups),
        out_shape=[jax.ShapeDtypeStruct((CHANNELS * BLK_DEV, voxels), jnp.float32)] * groups,
        in_specs=[in_vmem] * 3,
        out_specs=[in_vmem] * groups,
        scratch_shapes=[pltpu.VMEM((inner_rows, depth), jnp.bfloat16)],
        compiler_params=pltpu.CompilerParams(vmem_limit_bytes=VMEM_LIMIT),
        cost_estimate=pl.CostEstimate(
            flops=2 * inner_rows * depth * voxels, bytes_accessed=2 * depth * voxels, transcendentals=0
        ),
        name="inner",
    )(picked, meta, split)

    def to_owner(parts):
        return [
            lax.ppermute(parts[step], "frame", [(i, (i + step) % groups) for i in range(groups)])
            for step in range(1, groups)
        ]

    arrived = to_owner(edges)
    overhang = pl.pallas_call(
        sum_kernel,
        out_shape=jax.ShapeDtypeStruct((CHANNELS, voxels), jnp.float32),
        in_specs=[in_vmem] * groups,
        out_specs=in_vmem,
        compiler_params=pltpu.CompilerParams(vmem_limit_bytes=VMEM_LIMIT),
        cost_estimate=pl.CostEstimate(flops=10**9, bytes_accessed=0, transcendentals=0),
        name="sum_edges",
    )(edges[0], *arrived)
    received = to_owner(blocks)
    turn = [(i, i) for i in range(bricks, top * bricks)]
    for i in range(bricks):
        turn.append((i, i + 1 if i + 1 < bricks else top * bricks + i))
        turn.append((top * bricks + i, top * bricks + i - 1 if i else 0))
    handed = lax.ppermute(overhang, ("frame", "brick"), turn)
    merged, weight = pl.pallas_call(
        functools.partial(finish_kernel, groups),
        out_shape=[jax.ShapeDtypeStruct((BLK_DEV, voxels), jnp.float32)] * 2,
        in_specs=[in_vmem] * (groups + 1),
        out_specs=[in_vmem] * 2,
        compiler_params=pltpu.CompilerParams(vmem_limit_bytes=VMEM_LIMIT),
        name="finish",
    )(handed, blocks[0], *received)
    return (merged[None], weight[None])


def solution(mesh):
    placed = (
        P("frame", "brick", None),
        P("frame", "brick", None),
        P("frame", "brick", None, None, None),
        P("frame", "brick"),
        P("frame", "brick", None),
        P("frame", "brick", None),
    )
    return jax.shard_map(
        on_device,
        mesh=mesh,
        in_specs=placed,
        out_specs=(P("brick", "frame", None), P("brick", "frame", None)),
        check_vma=False,
    )
```

```python
import functools

import jax
import jax.numpy as jnp
from jax import lax
from jax.experimental import pallas as pl
from jax.experimental.pallas import tpu as pltpu
from jax.sharding import PartitionSpec as P

BLK_DEV = 16
CHANNELS = 2
VMEM_LIMIT = 8 * 1024 * 1024
BLOCK_ROWS = CHANNELS * BLK_DEV + 8


def join_kernel(spare, *refs):
    refs, out_ref, at = refs[:-1], refs[-1], 0
    for ref in refs if spare is None else refs[:-1]:
        out_ref[pl.ds(at, ref.shape[0])] = ref[...]
        at += ref.shape[0]
    if spare is not None:
        own = refs[-1]

        @pl.when(lax.axis_index("brick") % 2 == 0)
        def _():
            out_ref[pl.ds(spare * own.shape[0], own.shape[0])] = own[...]


def join(parts, spare=None):
    in_vmem = pl.BlockSpec(memory_space=pltpu.VMEM)
    count = sum(part.shape[0] for part in (parts if spare is None else parts[:-1]))
    return pl.pallas_call(
        functools.partial(join_kernel, spare),
        out_shape=jax.ShapeDtypeStruct((count,) + parts[0].shape[1:], parts[0].dtype),
        in_specs=[in_vmem] * len(parts),
        out_specs=in_vmem,
        compiler_params=pltpu.CompilerParams(vmem_limit_bytes=VMEM_LIMIT),
        cost_estimate=pl.CostEstimate(flops=10**11, bytes_accessed=0, transcendentals=0),
        name="join_rows",
    )(*parts)


def swap(rows, bricks, even, odd):
    return lax.ppermute(rows, "brick", [(i, i ^ (odd if i % 2 else even)) for i in range(bricks)])


def gather_half(rows, bricks):
    held = rows[None]
    if bricks == 16:
        held = jnp.concatenate([held, swap(held, bricks, 1, 1)], axis=0)
        even, odd, spare = (2, 4, 2), (8, 14, 10), 2
        arrived = {at: swap(held, bricks, even[at], odd[at]) for at in (0, 1, 2)}
        arrived = [arrived[at] for at in range(len(even))]
        handed = swap(arrived[0], bricks, 4, 4)
        even, odd = even + (even[0] ^ 4,), odd + (odd[0] ^ 4,)
        of_even = [d ^ c for at, d in enumerate(even) for d in (0 if at == spare else d,) for c in (0, 1)]
        of_odd = [d ^ c for d in odd for c in (0, 1)]
        of_even, of_odd = of_even + [d ^ 1 for d in of_odd], of_odd + [d ^ 1 for d in of_even]
        return join([join(arrived[:1])] + arrived[1:] + [handed, held], spare), of_even, of_odd
    parts, distances, step = [held], [0], bricks // 2
    while step > 1:
        arrived = swap(jnp.concatenate(parts, axis=0), bricks, step, step)
        parts, distances = parts + [arrived], distances + [d ^ step for d in distances]
        step //= 2
    distances = distances + [d ^ 1 for d in distances]
    return join(parts), distances, distances


def place_of(distance, distances):
    place = 0
    for at, d in enumerate(distances):
        place = place + jnp.where(distance == d, at, 0)
    return place


def prepare_kernel(of_even, of_odd, per_owner, block_rows, bricks, groups, slots, index_ref, meta_ref):
    brick, group = lax.axis_index("brick"), lax.axis_index("frame")
    frames = index_ref.shape[0]
    pair = slots * CHANNELS
    wide = (pair, meta_ref.shape[1])
    row = lax.broadcasted_iota(jnp.int32, wide, 0)
    channel = row % CHANNELS
    mine = lax.broadcasted_iota(jnp.int32, (pair, slots), 1) == (
        lax.broadcasted_iota(jnp.int32, (pair, slots), 0) // CHANNELS
    )
    for frame in range(frames):
        line = jnp.broadcast_to(index_ref[pl.ds(frame, 1), :], mine.shape)
        index = jnp.broadcast_to(jnp.sum(jnp.where(mine, line, 0), axis=1, keepdims=True), wide)
        pixel_block = index // (block_rows + 3)
        offset = index - pixel_block * (block_rows + 3)
        owner = pixel_block // per_owner
        place = jnp.where(brick % 2 == 0, place_of(owner ^ brick, of_even), place_of(owner ^ brick, of_odd))
        target = (place * CHANNELS + channel) * per_owner + (pixel_block - owner * per_owner)
        meta_ref[pl.ds(frame * pair, pair), :] = target
        low, high = offset == 0, offset == block_rows + 1
        holder = jnp.where(low, groups - 1, jnp.where(high, 0, (offset - 1) // BLK_DEV))
        step = holder - group
        step = jnp.where(step < 0, step + groups, step)
        inside = offset - 1 - holder * BLK_DEV + BLK_DEV * channel
        goal = step * BLOCK_ROWS + jnp.where(low | high, CHANNELS * BLK_DEV + channel, inside)
        live = offset < block_rows + 2
        live = live & ~(low & (brick == 0)) & ~(high & (brick == bricks - 1))
        meta_ref[pl.ds((frames + frame) * pair, pair), :] = jnp.where(live, goal, -1)


def edge_kernel(frames, slots, groups, near_ref, far_ref, meta_ref, split_ref, *refs):
    picked_ref, edges, placed_ref = refs[0], refs[1 : 1 + groups], refs[1 + groups]
    half, per_brick, pixels = near_ref.shape
    per_owner = per_brick // (CHANNELS * frames)
    reach = 2 * half * CHANNELS * per_owner
    pair = CHANNELS * slots
    lane = lax.broadcasted_iota(jnp.int32, (pair, pixels), 1)
    row = lax.broadcasted_iota(jnp.int32, (placed_ref.shape[0], pixels), 0)
    row = row // CHANNELS * BLOCK_ROWS + CHANNELS * BLK_DEV + row % CHANNELS
    for frame in range(frames):
        target = meta_ref[pl.ds(frame * pair, pair), :]
        chosen = jnp.concatenate(
            [(target == lane + start).astype(jnp.float32) for start in range(0, reach, pixels)], axis=1
        ).astype(jnp.bfloat16)
        own = jnp.concatenate(
            [
                jnp.concatenate(
                    [ref[:, pl.ds((c * frames + frame) * per_owner, per_owner), :] for c in range(CHANNELS)],
                    axis=1,
                ).reshape(reach // 2, pixels)
                for ref in (near_ref, far_ref)
            ],
            axis=0,
        )
        picked = jnp.dot(chosen, own, preferred_element_type=jnp.float32)
        picked_ref[pl.ds(frame * pair, pair), :] = picked
        goal = meta_ref[pl.ds((frames + frame) * pair, pair), :]
        for slot in range(slots):
            laid = jnp.zeros(row.shape, jnp.float32)
            for c in range(CHANNELS):
                at = CHANNELS * slot + c
                value = jnp.broadcast_to(picked[at : at + 1], row.shape)
                laid = jnp.where(row == jnp.broadcast_to(goal[at : at + 1], row.shape), value, laid)
            place = (frame * slots + slot) * pixels
            placed_ref[:, pl.ds(place, pixels)] = laid.astype(jnp.bfloat16)
    total = jnp.dot(placed_ref[...], split_ref[...], preferred_element_type=jnp.float32)
    for block in range(groups):
        edges[block][...] = total[CHANNELS * block : CHANNELS * (block + 1)]


def inner_kernel(frames, slots, groups, picked_ref, meta_ref, split_ref, *refs):
    inner, placed_ref = refs[:groups], refs[groups]
    pixels = picked_ref.shape[1]
    pair = CHANNELS * slots
    row = lax.broadcasted_iota(jnp.int32, (BLK_DEV, pixels), 0)
    zero = jnp.zeros(row.shape, jnp.float32)
    for frame in range(frames):
        picked = picked_ref[pl.ds(frame * pair, pair), :]
        goal = meta_ref[pl.ds((frames + frame) * pair, pair), :]
        for slot in range(slots):
            parts = []
            for block in range(groups):
                for c in range(CHANNELS):
                    at = CHANNELS * slot + c
                    value = jnp.broadcast_to(picked[at : at + 1], row.shape)
                    here = jnp.broadcast_to(goal[at : at + 1], row.shape) - (block * BLOCK_ROWS + c * BLK_DEV)
                    parts.append(jnp.where(row == here, value, zero))
            place = (frame * slots + slot) * pixels
            placed_ref[:, pl.ds(place, pixels)] = jnp.concatenate(parts, axis=0).astype(jnp.bfloat16)
    total = jnp.dot(placed_ref[...], split_ref[...], preferred_element_type=jnp.float32)
    for block in range(groups):
        base = block * CHANNELS * BLK_DEV
        inner[block][...] = total[base : base + CHANNELS * BLK_DEV]


def sum_kernel(*refs):
    total = refs[0][...]
    for ref in refs[1:-1]:
        total = total + ref[...]
    refs[-1][...] = total


def finish_kernel(groups, handed_ref, *refs):
    parts, (merged_ref, weight_ref) = refs[:groups], refs[groups:]
    group = lax.axis_index("frame")
    row = jnp.where(group == 0, 0, jnp.where(group == groups - 1, BLK_DEV - 1, -1))
    here = lax.broadcasted_iota(jnp.int32, merged_ref.shape, 0) == row
    totals = []
    for c in range(CHANNELS):
        rows = pl.ds(c * BLK_DEV, BLK_DEV)
        total = jnp.where(here, handed_ref[pl.ds(c, 1), :], 0.0)
        for part in parts:
            total = total + part[rows, :]
        totals.append(total)
    weight_ref[...] = totals[1]
    merged_ref[...] = totals[0] / jnp.maximum(totals[1], 1.0)


def on_device(intensity, correction, splitting, block_count, pix_index, vox_offset):
    frames_dev, blocks_per_device, pixel_width = intensity.shape
    max_slots = splitting.shape[2]
    voxels = splitting.shape[4]
    bricks = lax.axis_size("brick")
    groups = lax.axis_size("frame")
    top = groups - 1
    block_rows = BLK_DEV * groups
    slot_count = frames_dev * max_slots

    in_vmem = pl.BlockSpec(memory_space=pltpu.VMEM)
    row_count = frames_dev * blocks_per_device
    local_rows = jnp.stack([intensity, correction], axis=0).astype(jnp.bfloat16)
    local_rows = local_rows.reshape(CHANNELS * row_count, pixel_width)
    depth = slot_count * pixel_width

    split = splitting.reshape(depth, voxels)

    near, of_even, of_odd = gather_half(local_rows, bricks)
    near, block_count, pix_index, vox_offset = lax.optimization_barrier(
        (near, block_count, pix_index, vox_offset)
    )
    far = swap(near, bricks, 1, 1)
    live = jnp.arange(max_slots, dtype=jnp.int32) < block_count[:, :, None]
    index = pix_index * (block_rows + 3) + jnp.where(live, vox_offset, block_rows + 2)
    meta = pl.pallas_call(
        functools.partial(
            prepare_kernel, of_even, of_odd, blocks_per_device, block_rows, bricks, groups, max_slots
        ),
        out_shape=jax.ShapeDtypeStruct((2 * CHANNELS * slot_count, pixel_width), jnp.int32),
        in_specs=[in_vmem],
        out_specs=in_vmem,
        compiler_params=pltpu.CompilerParams(vmem_limit_bytes=VMEM_LIMIT),
        name="prepare",
    )(index.reshape(frames_dev, max_slots))

    edge_rows = -(-CHANNELS * groups // 16) * 16
    inner_rows = CHANNELS * BLK_DEV * groups
    picked, *edges = pl.pallas_call(
        functools.partial(edge_kernel, frames_dev, max_slots, groups),
        out_shape=[jax.ShapeDtypeStruct((CHANNELS * slot_count, pixel_width), jnp.float32)]
        + [jax.ShapeDtypeStruct((CHANNELS, voxels), jnp.float32)] * groups,
        in_specs=[in_vmem] * 4,
        out_specs=[in_vmem] * (1 + groups),
        scratch_shapes=[pltpu.VMEM((edge_rows, depth), jnp.bfloat16)],
        compiler_params=pltpu.CompilerParams(vmem_limit_bytes=VMEM_LIMIT),
        cost_estimate=pl.CostEstimate(
            flops=2 * edge_rows * depth * voxels, bytes_accessed=2 * depth * voxels, transcendentals=0
        ),
        name="edges",
    )(near, far, meta, split)
    blocks = pl.pallas_call(
        functools.partial(inner_kernel, frames_dev, max_slots, groups),
        out_shape=[jax.ShapeDtypeStruct((CHANNELS * BLK_DEV, voxels), jnp.float32)] * groups,
        in_specs=[in_vmem] * 3,
        out_specs=[in_vmem] * groups,
        scratch_shapes=[pltpu.VMEM((inner_rows, depth), jnp.bfloat16)],
        compiler_params=pltpu.CompilerParams(vmem_limit_bytes=VMEM_LIMIT),
        cost_estimate=pl.CostEstimate(
            flops=2 * inner_rows * depth * voxels, bytes_accessed=2 * depth * voxels, transcendentals=0
        ),
        name="inner",
    )(picked, meta, split)

    def to_owner(parts):
        return [
            lax.ppermute(parts[step], "frame", [(i, (i + step) % groups) for i in range(groups)])
            for step in range(1, groups)
        ]

    arrived = to_owner(edges)
    overhang = pl.pallas_call(
        sum_kernel,
        out_shape=jax.ShapeDtypeStruct((CHANNELS, voxels), jnp.float32),
        in_specs=[in_vmem] * groups,
        out_specs=in_vmem,
        compiler_params=pltpu.CompilerParams(vmem_limit_bytes=VMEM_LIMIT),
        cost_estimate=pl.CostEstimate(flops=10**9, bytes_accessed=0, transcendentals=0),
        name="sum_edges",
    )(edges[0], *arrived)
    received = to_owner(blocks)
    turn = [(i, i) for i in range(bricks, top * bricks)]
    for i in range(bricks):
        turn.append((i, i + 1 if i + 1 < bricks else top * bricks + i))
        turn.append((top * bricks + i, top * bricks + i - 1 if i else 0))
    handed = lax.ppermute(overhang, ("frame", "brick"), turn)
    merged, weight = pl.pallas_call(
        functools.partial(finish_kernel, groups),
        out_shape=[jax.ShapeDtypeStruct((BLK_DEV, voxels), jnp.float32)] * 2,
        in_specs=[in_vmem] * (groups + 1),
        out_specs=[in_vmem] * 2,
        compiler_params=pltpu.CompilerParams(vmem_limit_bytes=VMEM_LIMIT),
        name="finish",
    )(handed, blocks[0], *received)
    return (merged[None], weight[None])


def solution(mesh):
    placed = (
        P("frame", "brick", None),
        P("frame", "brick", None),
        P("frame", "brick", None, None, None),
        P("frame", "brick"),
        P("frame", "brick", None),
        P("frame", "brick", None),
    )
    return jax.shard_map(
        on_device,
        mesh=mesh,
        in_specs=placed,
        out_specs=(P("brick", "frame", None), P("brick", "frame", None)),
        check_vma=False,
    )
```

```python
import functools

import jax
import jax.numpy as jnp
from jax import lax
from jax.experimental import pallas as pl
from jax.experimental.pallas import tpu as pltpu
from jax.sharding import PartitionSpec as P

BLK_DEV = 16
CHANNELS = 2
VMEM_LIMIT = 8 * 1024 * 1024
BLOCK_ROWS = CHANNELS * BLK_DEV + 8


def join_kernel(spare, *refs):
    refs, out_ref, at = refs[:-1], refs[-1], 0
    for ref in refs if spare is None else refs[:-1]:
        out_ref[pl.ds(at, ref.shape[0])] = ref[...]
        at += ref.shape[0]
    if spare is not None:
        own = refs[-1]

        @pl.when(lax.axis_index("brick") % 2 == 0)
        def _():
            out_ref[pl.ds(spare * own.shape[0], own.shape[0])] = own[...]


def join(parts, spare=None):
    in_vmem = pl.BlockSpec(memory_space=pltpu.VMEM)
    count = sum(part.shape[0] for part in (parts if spare is None else parts[:-1]))
    return pl.pallas_call(
        functools.partial(join_kernel, spare),
        out_shape=jax.ShapeDtypeStruct((count,) + parts[0].shape[1:], parts[0].dtype),
        in_specs=[in_vmem] * len(parts),
        out_specs=in_vmem,
        compiler_params=pltpu.CompilerParams(vmem_limit_bytes=VMEM_LIMIT),
        cost_estimate=pl.CostEstimate(flops=10**11, bytes_accessed=0, transcendentals=0),
        name="join_rows",
    )(*parts)


def swap(rows, bricks, even, odd):
    return lax.ppermute(rows, "brick", [(i, i ^ (odd if i % 2 else even)) for i in range(bricks)])


def pair_kernel(own_ref, *refs):
    refs, out_ref = refs[:-1], refs[-1]
    out_ref[0] = own_ref[...]
    for at, ref in enumerate(refs):
        out_ref[1, pl.ds(at * ref.shape[0], ref.shape[0]), :] = ref[...].astype(jnp.bfloat16)


def pair_up(own, others):
    in_vmem = pl.BlockSpec(memory_space=pltpu.VMEM)
    return pl.pallas_call(
        pair_kernel,
        out_shape=jax.ShapeDtypeStruct((2,) + own.shape, own.dtype),
        in_specs=[in_vmem] * (1 + len(others)),
        out_specs=in_vmem,
        compiler_params=pltpu.CompilerParams(vmem_limit_bytes=VMEM_LIMIT),
        name="pair_rows",
    )(own, *others)


def gather_half(rows, exact, bricks):
    held = rows[None]
    if bricks == 16:
        held = pair_up(rows, [swap(part, bricks, 1, 1) for part in exact])
        even, odd, spare = (2, 2, 4), (8, 12, 14), 1
        arrived = {at: swap(held, bricks, even[at], odd[at]) for at in (0, 1, 2)}
        arrived = [arrived[at] for at in range(len(even))]
        handed = swap(arrived[0], bricks, 4, 2)
        even, odd = even + (even[0] ^ 4,), odd + (odd[0] ^ 2,)
        of_even = [d ^ c for at, d in enumerate(even) for d in (0 if at == spare else d,) for c in (0, 1)]
        of_odd = [d ^ c for d in odd for c in (0, 1)]
        of_even, of_odd = of_even + [d ^ 1 for d in of_odd], of_odd + [d ^ 1 for d in of_even]
        return join([join(arrived[:1])] + arrived[1:] + [handed, held], spare), of_even, of_odd
    parts, distances, step = [held], [0], bricks // 2
    while step > 1:
        arrived = swap(jnp.concatenate(parts, axis=0), bricks, step, step)
        parts, distances = parts + [arrived], distances + [d ^ step for d in distances]
        step //= 2
    distances = distances + [d ^ 1 for d in distances]
    return join(parts), distances, distances


def place_of(distance, distances):
    place = 0
    for at, d in enumerate(distances):
        place = place + jnp.where(distance == d, at, 0)
    return place


def prepare_kernel(of_even, of_odd, per_owner, block_rows, bricks, groups, slots, index_ref, meta_ref):
    brick, group = lax.axis_index("brick"), lax.axis_index("frame")
    frames = index_ref.shape[0]
    pair = slots * CHANNELS
    wide = (pair, meta_ref.shape[1])
    row = lax.broadcasted_iota(jnp.int32, wide, 0)
    channel = row % CHANNELS
    mine = lax.broadcasted_iota(jnp.int32, (pair, slots), 1) == (
        lax.broadcasted_iota(jnp.int32, (pair, slots), 0) // CHANNELS
    )
    for frame in range(frames):
        line = jnp.broadcast_to(index_ref[pl.ds(frame, 1), :], mine.shape)
        index = jnp.broadcast_to(jnp.sum(jnp.where(mine, line, 0), axis=1, keepdims=True), wide)
        pixel_block = index // (block_rows + 3)
        offset = index - pixel_block * (block_rows + 3)
        owner = pixel_block // per_owner
        place = jnp.where(brick % 2 == 0, place_of(owner ^ brick, of_even), place_of(owner ^ brick, of_odd))
        target = (place * CHANNELS + channel) * per_owner + (pixel_block - owner * per_owner)
        meta_ref[pl.ds(frame * pair, pair), :] = target
        low, high = offset == 0, offset == block_rows + 1
        holder = jnp.where(low, groups - 1, jnp.where(high, 0, (offset - 1) // BLK_DEV))
        step = holder - group
        step = jnp.where(step < 0, step + groups, step)
        inside = offset - 1 - holder * BLK_DEV + BLK_DEV * channel
        goal = step * BLOCK_ROWS + jnp.where(low | high, CHANNELS * BLK_DEV + channel, inside)
        live = offset < block_rows + 2
        live = live & ~(low & (brick == 0)) & ~(high & (brick == bricks - 1))
        meta_ref[pl.ds((frames + frame) * pair, pair), :] = jnp.where(live, goal, -1)


def pick(frames, slots, frame, start, rows_ref, meta_ref):
    count, per_brick, pixels = rows_ref.shape
    per_owner = per_brick // (CHANNELS * frames)
    reach = count * CHANNELS * per_owner
    pair = CHANNELS * slots
    lane = lax.broadcasted_iota(jnp.int32, (pair, pixels), 1) + start * CHANNELS * per_owner
    target = meta_ref[pl.ds(frame * pair, pair), :]
    chosen = jnp.concatenate(
        [(target == lane + at).astype(jnp.float32) for at in range(0, reach, pixels)], axis=1
    ).astype(jnp.bfloat16)
    own = jnp.concatenate(
        [rows_ref[:, pl.ds((c * frames + frame) * per_owner, per_owner), :] for c in range(CHANNELS)], axis=1
    )
    return jnp.dot(chosen, own.reshape(reach, pixels), preferred_element_type=jnp.float32)


def pick_kernel(frames, slots, near_ref, meta_ref, picked_ref):
    pair = CHANNELS * slots
    for frame in range(frames):
        picked_ref[pl.ds(frame * pair, pair), :] = pick(frames, slots, frame, 0, near_ref, meta_ref)


def edge_kernel(frames, slots, groups, early_ref, far_ref, meta_ref, split_ref, *refs):
    picked_ref, edges, placed_ref = refs[0], refs[1 : 1 + groups], refs[1 + groups]
    half, _, pixels = far_ref.shape
    pair = CHANNELS * slots
    row = lax.broadcasted_iota(jnp.int32, (placed_ref.shape[0], pixels), 0)
    row = row // CHANNELS * BLOCK_ROWS + CHANNELS * BLK_DEV + row % CHANNELS
    for frame in range(frames):
        picked = early_ref[pl.ds(frame * pair, pair), :]
        picked = picked + pick(frames, slots, frame, half, far_ref, meta_ref)
        picked_ref[pl.ds(frame * pair, pair), :] = picked
        goal = meta_ref[pl.ds((frames + frame) * pair, pair), :]
        for slot in range(slots):
            laid = jnp.zeros(row.shape, jnp.float32)
            for c in range(CHANNELS):
                at = CHANNELS * slot + c
                value = jnp.broadcast_to(picked[at : at + 1], row.shape)
                laid = jnp.where(row == jnp.broadcast_to(goal[at : at + 1], row.shape), value, laid)
            place = (frame * slots + slot) * pixels
            placed_ref[:, pl.ds(place, pixels)] = laid.astype(jnp.bfloat16)
    total = jnp.dot(placed_ref[...], split_ref[...], preferred_element_type=jnp.float32)
    for block in range(groups):
        edges[block][...] = total[CHANNELS * block : CHANNELS * (block + 1)]


def inner_kernel(frames, slots, groups, picked_ref, meta_ref, split_ref, *refs):
    inner, placed_ref = refs[:groups], refs[groups]
    pixels = picked_ref.shape[1]
    pair = CHANNELS * slots
    row = lax.broadcasted_iota(jnp.int32, (BLK_DEV, pixels), 0)
    zero = jnp.zeros(row.shape, jnp.float32)
    for frame in range(frames):
        picked = picked_ref[pl.ds(frame * pair, pair), :]
        goal = meta_ref[pl.ds((frames + frame) * pair, pair), :]
        for slot in range(slots):
            parts = []
            for block in range(groups):
                for c in range(CHANNELS):
                    at = CHANNELS * slot + c
                    value = jnp.broadcast_to(picked[at : at + 1], row.shape)
                    here = jnp.broadcast_to(goal[at : at + 1], row.shape) - (block * BLOCK_ROWS + c * BLK_DEV)
                    parts.append(jnp.where(row == here, value, zero))
            place = (frame * slots + slot) * pixels
            placed_ref[:, pl.ds(place, pixels)] = jnp.concatenate(parts, axis=0).astype(jnp.bfloat16)
    total = jnp.dot(placed_ref[...], split_ref[...], preferred_element_type=jnp.float32)
    for block in range(groups):
        base = block * CHANNELS * BLK_DEV
        inner[block][...] = total[base : base + CHANNELS * BLK_DEV]


def sum_kernel(*refs):
    total = refs[0][...]
    for ref in refs[1:-1]:
        total = total + ref[...]
    refs[-1][...] = total


def finish_kernel(groups, handed_ref, *refs):
    parts, (merged_ref, weight_ref) = refs[:groups], refs[groups:]
    group = lax.axis_index("frame")
    row = jnp.where(group == 0, 0, jnp.where(group == groups - 1, BLK_DEV - 1, -1))
    here = lax.broadcasted_iota(jnp.int32, merged_ref.shape, 0) == row
    totals = []
    for c in range(CHANNELS):
        rows = pl.ds(c * BLK_DEV, BLK_DEV)
        total = jnp.where(here, handed_ref[pl.ds(c, 1), :], 0.0)
        for part in parts:
            total = total + part[rows, :]
        totals.append(total)
    weight_ref[...] = totals[1]
    merged_ref[...] = totals[0] / jnp.maximum(totals[1], 1.0)


def on_device(intensity, correction, splitting, block_count, pix_index, vox_offset):
    frames_dev, blocks_per_device, pixel_width = intensity.shape
    max_slots = splitting.shape[2]
    voxels = splitting.shape[4]
    bricks = lax.axis_size("brick")
    groups = lax.axis_size("frame")
    top = groups - 1
    block_rows = BLK_DEV * groups
    slot_count = frames_dev * max_slots

    in_vmem = pl.BlockSpec(memory_space=pltpu.VMEM)
    row_count = frames_dev * blocks_per_device
    exact = [part.reshape(row_count, pixel_width) for part in (intensity, correction)]
    local_rows = jnp.pad(exact[0], ((0, row_count), (0, 0))) + jnp.pad(exact[1], ((row_count, 0), (0, 0)))
    local_rows = local_rows.astype(jnp.bfloat16)
    depth = slot_count * pixel_width

    split = splitting.reshape(depth, voxels)

    near, of_even, of_odd = gather_half(local_rows, exact, bricks)
    near, block_count, pix_index, vox_offset = lax.optimization_barrier(
        (near, block_count, pix_index, vox_offset)
    )
    far = swap(near, bricks, 1, 1)
    live = jnp.arange(max_slots, dtype=jnp.int32) < block_count[:, :, None]
    index = pix_index * (block_rows + 3) + jnp.where(live, vox_offset, block_rows + 2)
    meta = pl.pallas_call(
        functools.partial(
            prepare_kernel, of_even, of_odd, blocks_per_device, block_rows, bricks, groups, max_slots
        ),
        out_shape=jax.ShapeDtypeStruct((2 * CHANNELS * slot_count, pixel_width), jnp.int32),
        in_specs=[in_vmem],
        out_specs=in_vmem,
        compiler_params=pltpu.CompilerParams(vmem_limit_bytes=VMEM_LIMIT),
        name="prepare",
    )(index.reshape(frames_dev, max_slots))

    early = pl.pallas_call(
        functools.partial(pick_kernel, frames_dev, max_slots),
        out_shape=jax.ShapeDtypeStruct((CHANNELS * slot_count, pixel_width), jnp.float32),
        in_specs=[in_vmem] * 2,
        out_specs=in_vmem,
        compiler_params=pltpu.CompilerParams(vmem_limit_bytes=VMEM_LIMIT),
        name="pick_near",
    )(near, meta)
    edge_rows = -(-CHANNELS * groups // 16) * 16
    inner_rows = CHANNELS * BLK_DEV * groups
    picked, *edges = pl.pallas_call(
        functools.partial(edge_kernel, frames_dev, max_slots, groups),
        out_shape=[jax.ShapeDtypeStruct((CHANNELS * slot_count, pixel_width), jnp.float32)]
        + [jax.ShapeDtypeStruct((CHANNELS, voxels), jnp.float32)] * groups,
        in_specs=[in_vmem] * 4,
        out_specs=[in_vmem] * (1 + groups),
        scratch_shapes=[pltpu.VMEM((edge_rows, depth), jnp.bfloat16)],
        compiler_params=pltpu.CompilerParams(vmem_limit_bytes=VMEM_LIMIT),
        cost_estimate=pl.CostEstimate(
            flops=2 * edge_rows * depth * voxels, bytes_accessed=2 * depth * voxels, transcendentals=0
        ),
        name="edges",
    )(early, far, meta, split)
    blocks = pl.pallas_call(
        functools.partial(inner_kernel, frames_dev, max_slots, groups),
        out_shape=[jax.ShapeDtypeStruct((CHANNELS * BLK_DEV, voxels), jnp.float32)] * groups,
        in_specs=[in_vmem] * 3,
        out_specs=[in_vmem] * groups,
        scratch_shapes=[pltpu.VMEM((inner_rows, depth), jnp.bfloat16)],
        compiler_params=pltpu.CompilerParams(vmem_limit_bytes=VMEM_LIMIT),
        cost_estimate=pl.CostEstimate(
            flops=2 * inner_rows * depth * voxels, bytes_accessed=2 * depth * voxels, transcendentals=0
        ),
        name="inner",
    )(picked, meta, split)

    def to_owner(parts):
        return [
            lax.ppermute(parts[step], "frame", [(i, (i + step) % groups) for i in range(groups)])
            for step in range(1, groups)
        ]

    arrived = to_owner(edges)
    overhang = pl.pallas_call(
        sum_kernel,
        out_shape=jax.ShapeDtypeStruct((CHANNELS, voxels), jnp.float32),
        in_specs=[in_vmem] * groups,
        out_specs=in_vmem,
        compiler_params=pltpu.CompilerParams(vmem_limit_bytes=VMEM_LIMIT),
        cost_estimate=pl.CostEstimate(flops=10**9, bytes_accessed=0, transcendentals=0),
        name="sum_edges",
    )(edges[0], *arrived)
    received = to_owner(blocks)
    turn = [(i, i) for i in range(bricks, top * bricks)]
    for i in range(bricks):
        turn.append((i, i + 1 if i + 1 < bricks else top * bricks + i))
        turn.append((top * bricks + i, top * bricks + i - 1 if i else 0))
    handed = lax.ppermute(overhang, ("frame", "brick"), turn)
    merged, weight = pl.pallas_call(
        functools.partial(finish_kernel, groups),
        out_shape=[jax.ShapeDtypeStruct((BLK_DEV, voxels), jnp.float32)] * 2,
        in_specs=[in_vmem] * (groups + 1),
        out_specs=[in_vmem] * 2,
        compiler_params=pltpu.CompilerParams(vmem_limit_bytes=VMEM_LIMIT),
        name="finish",
    )(handed, blocks[0], *received)
    return (merged[None], weight[None])


def solution(mesh):
    placed = (
        P("frame", "brick", None),
        P("frame", "brick", None),
        P("frame", "brick", None, None, None),
        P("frame", "brick"),
        P("frame", "brick", None),
        P("frame", "brick", None),
    )
    return jax.shard_map(
        on_device,
        mesh=mesh,
        in_specs=placed,
        out_specs=(P("brick", "frame", None), P("brick", "frame", None)),
        check_vma=False,
    )
```

```python
import functools

import jax
import jax.numpy as jnp
from jax import lax
from jax.experimental import pallas as pl
from jax.experimental.pallas import tpu as pltpu
from jax.sharding import PartitionSpec as P

BLK_DEV = 16
CHANNELS = 2
VMEM_LIMIT = 8 * 1024 * 1024
BLOCK_ROWS = CHANNELS * BLK_DEV + 8


def join_kernel(spare, *refs):
    refs, out_ref, at = refs[:-1], refs[-1], 0
    for ref in refs if spare is None else refs[:-1]:
        out_ref[pl.ds(at, ref.shape[0])] = ref[...]
        at += ref.shape[0]
    if spare is not None:
        own = refs[-1]

        @pl.when(lax.axis_index("brick") % 2 == 0)
        def _():
            out_ref[pl.ds(spare * own.shape[0], own.shape[0])] = own[...]


def join(parts, spare=None):
    in_vmem = pl.BlockSpec(memory_space=pltpu.VMEM)
    count = sum(part.shape[0] for part in (parts if spare is None else parts[:-1]))
    return pl.pallas_call(
        functools.partial(join_kernel, spare),
        out_shape=jax.ShapeDtypeStruct((count,) + parts[0].shape[1:], parts[0].dtype),
        in_specs=[in_vmem] * len(parts),
        out_specs=in_vmem,
        compiler_params=pltpu.CompilerParams(vmem_limit_bytes=VMEM_LIMIT),
        cost_estimate=pl.CostEstimate(flops=10**11, bytes_accessed=0, transcendentals=0),
        name="join_rows",
    )(*parts)


def swap(rows, bricks, even, odd):
    return lax.ppermute(rows, "brick", [(i, i ^ (odd if i % 2 else even)) for i in range(bricks)])


def pair_kernel(own_ref, *refs):
    refs, out_ref = refs[:-1], refs[-1]
    out_ref[0] = own_ref[...]
    for at, ref in enumerate(refs):
        out_ref[1, pl.ds(at * ref.shape[0], ref.shape[0]), :] = ref[...].astype(jnp.bfloat16)


def pair_up(own, others):
    in_vmem = pl.BlockSpec(memory_space=pltpu.VMEM)
    return pl.pallas_call(
        pair_kernel,
        out_shape=jax.ShapeDtypeStruct((2,) + own.shape, own.dtype),
        in_specs=[in_vmem] * (1 + len(others)),
        out_specs=in_vmem,
        compiler_params=pltpu.CompilerParams(vmem_limit_bytes=VMEM_LIMIT),
        name="pair_rows",
    )(own, *others)


def gather_half(rows, exact, bricks):
    held = rows[None]
    if bricks == 16:
        held = pair_up(rows, [swap(part, bricks, 1, 1) for part in exact])
        even, odd, spare = (2, 4, 2), (8, 14, 12), 2
        arrived = {at: swap(held, bricks, even[at], odd[at]) for at in (0, 1, 2)}
        arrived = [arrived[at] for at in range(len(even))]
        handed = swap(arrived[0], bricks, 4, 2)
        even, odd = even + (even[0] ^ 4,), odd + (odd[0] ^ 2,)
        of_even = [d ^ c for at, d in enumerate(even) for d in (0 if at == spare else d,) for c in (0, 1)]
        of_odd = [d ^ c for d in odd for c in (0, 1)]
        of_even, of_odd = of_even + [d ^ 1 for d in of_odd], of_odd + [d ^ 1 for d in of_even]
        return [join(arrived[:2]), join([arrived[2], handed, held], 0)], of_even, of_odd
    parts, distances, step = [held], [0], bricks // 2
    while step > 1:
        arrived = swap(jnp.concatenate(parts, axis=0), bricks, step, step)
        parts, distances = parts + [arrived], distances + [d ^ step for d in distances]
        step //= 2
    distances = distances + [d ^ 1 for d in distances]
    return [join(parts)], distances, distances


def place_of(distance, distances):
    place = 0
    for at, d in enumerate(distances):
        place = place + jnp.where(distance == d, at, 0)
    return place


def prepare_kernel(of_even, of_odd, per_owner, block_rows, bricks, groups, slots, index_ref, meta_ref):
    brick, group = lax.axis_index("brick"), lax.axis_index("frame")
    frames = index_ref.shape[0]
    pair = slots * CHANNELS
    wide = (pair, meta_ref.shape[1])
    row = lax.broadcasted_iota(jnp.int32, wide, 0)
    channel = row % CHANNELS
    mine = lax.broadcasted_iota(jnp.int32, (pair, slots), 1) == (
        lax.broadcasted_iota(jnp.int32, (pair, slots), 0) // CHANNELS
    )
    for frame in range(frames):
        line = jnp.broadcast_to(index_ref[pl.ds(frame, 1), :], mine.shape)
        index = jnp.broadcast_to(jnp.sum(jnp.where(mine, line, 0), axis=1, keepdims=True), wide)
        pixel_block = index // (block_rows + 3)
        offset = index - pixel_block * (block_rows + 3)
        owner = pixel_block // per_owner
        place = jnp.where(brick % 2 == 0, place_of(owner ^ brick, of_even), place_of(owner ^ brick, of_odd))
        target = (place * CHANNELS + channel) * per_owner + (pixel_block - owner * per_owner)
        meta_ref[pl.ds(frame * pair, pair), :] = target
        low, high = offset == 0, offset == block_rows + 1
        holder = jnp.where(low, groups - 1, jnp.where(high, 0, (offset - 1) // BLK_DEV))
        step = holder - group
        step = jnp.where(step < 0, step + groups, step)
        inside = offset - 1 - holder * BLK_DEV + BLK_DEV * channel
        goal = step * BLOCK_ROWS + jnp.where(low | high, CHANNELS * BLK_DEV + channel, inside)
        live = offset < block_rows + 2
        live = live & ~(low & (brick == 0)) & ~(high & (brick == bricks - 1))
        meta_ref[pl.ds((frames + frame) * pair, pair), :] = jnp.where(live, goal, -1)


def pick(frames, slots, frame, start, rows_ref, meta_ref):
    count, per_brick, pixels = rows_ref.shape
    per_owner = per_brick // (CHANNELS * frames)
    reach = count * CHANNELS * per_owner
    pair = CHANNELS * slots
    lane = lax.broadcasted_iota(jnp.int32, (pair, pixels), 1) + start * CHANNELS * per_owner
    target = meta_ref[pl.ds(frame * pair, pair), :]
    chosen = jnp.concatenate(
        [(target == lane + at).astype(jnp.float32) for at in range(0, reach, pixels)], axis=1
    ).astype(jnp.bfloat16)
    own = jnp.concatenate(
        [rows_ref[:, pl.ds((c * frames + frame) * per_owner, per_owner), :] for c in range(CHANNELS)], axis=1
    )
    return jnp.dot(chosen, own.reshape(reach, pixels), preferred_element_type=jnp.float32)


def pick_all(frames, slots, frame, start, refs, meta_ref):
    total = 0.0
    for ref in refs:
        total = total + pick(frames, slots, frame, start, ref, meta_ref)
        start += ref.shape[0]
    return total


def pick_kernel(frames, slots, *refs):
    near, (meta_ref, picked_ref) = refs[:-2], refs[-2:]
    pair = CHANNELS * slots
    for frame in range(frames):
        picked_ref[pl.ds(frame * pair, pair), :] = pick_all(frames, slots, frame, 0, near, meta_ref)


def edge_kernel(frames, slots, groups, count, early_ref, *refs):
    far, (meta_ref, split_ref), refs = refs[:count], refs[count : count + 2], refs[count + 2 :]
    picked_ref, edges, placed_ref = refs[0], refs[1 : 1 + groups], refs[1 + groups]
    half, pixels = sum(ref.shape[0] for ref in far), far[0].shape[2]
    pair = CHANNELS * slots
    row = lax.broadcasted_iota(jnp.int32, (placed_ref.shape[0], pixels), 0)
    row = row // CHANNELS * BLOCK_ROWS + CHANNELS * BLK_DEV + row % CHANNELS
    for frame in range(frames):
        picked = early_ref[pl.ds(frame * pair, pair), :]
        picked = picked + pick_all(frames, slots, frame, half, far, meta_ref)
        picked_ref[pl.ds(frame * pair, pair), :] = picked
        goal = meta_ref[pl.ds((frames + frame) * pair, pair), :]
        for slot in range(slots):
            laid = jnp.zeros(row.shape, jnp.float32)
            for c in range(CHANNELS):
                at = CHANNELS * slot + c
                value = jnp.broadcast_to(picked[at : at + 1], row.shape)
                laid = jnp.where(row == jnp.broadcast_to(goal[at : at + 1], row.shape), value, laid)
            place = (frame * slots + slot) * pixels
            placed_ref[:, pl.ds(place, pixels)] = laid.astype(jnp.bfloat16)
    total = jnp.dot(placed_ref[...], split_ref[...], preferred_element_type=jnp.float32)
    for block in range(groups):
        edges[block][...] = total[CHANNELS * block : CHANNELS * (block + 1)]


def inner_kernel(frames, slots, groups, picked_ref, meta_ref, split_ref, *refs):
    inner, placed_ref = refs[:groups], refs[groups]
    pixels = picked_ref.shape[1]
    pair = CHANNELS * slots
    row = lax.broadcasted_iota(jnp.int32, (BLK_DEV, pixels), 0)
    zero = jnp.zeros(row.shape, jnp.float32)
    for frame in range(frames):
        picked = picked_ref[pl.ds(frame * pair, pair), :]
        goal = meta_ref[pl.ds((frames + frame) * pair, pair), :]
        for slot in range(slots):
            parts = []
            for block in range(groups):
                for c in range(CHANNELS):
                    at = CHANNELS * slot + c
                    value = jnp.broadcast_to(picked[at : at + 1], row.shape)
                    here = jnp.broadcast_to(goal[at : at + 1], row.shape) - (block * BLOCK_ROWS + c * BLK_DEV)
                    parts.append(jnp.where(row == here, value, zero))
            place = (frame * slots + slot) * pixels
            placed_ref[:, pl.ds(place, pixels)] = jnp.concatenate(parts, axis=0).astype(jnp.bfloat16)
    total = jnp.dot(placed_ref[...], split_ref[...], preferred_element_type=jnp.float32)
    for block in range(groups):
        base = block * CHANNELS * BLK_DEV
        inner[block][...] = total[base : base + CHANNELS * BLK_DEV]


def sum_kernel(*refs):
    total = refs[0][...]
    for ref in refs[1:-1]:
        total = total + ref[...]
    refs[-1][...] = total


def finish_kernel(groups, handed_ref, *refs):
    parts, (merged_ref, weight_ref) = refs[:groups], refs[groups:]
    group = lax.axis_index("frame")
    row = jnp.where(group == 0, 0, jnp.where(group == groups - 1, BLK_DEV - 1, -1))
    here = lax.broadcasted_iota(jnp.int32, merged_ref.shape, 0) == row
    totals = []
    for c in range(CHANNELS):
        rows = pl.ds(c * BLK_DEV, BLK_DEV)
        total = jnp.where(here, handed_ref[pl.ds(c, 1), :], 0.0)
        for part in parts:
            total = total + part[rows, :]
        totals.append(total)
    weight_ref[...] = totals[1]
    merged_ref[...] = totals[0] / jnp.maximum(totals[1], 1.0)


def on_device(intensity, correction, splitting, block_count, pix_index, vox_offset):
    frames_dev, blocks_per_device, pixel_width = intensity.shape
    max_slots = splitting.shape[2]
    voxels = splitting.shape[4]
    bricks = lax.axis_size("brick")
    groups = lax.axis_size("frame")
    top = groups - 1
    block_rows = BLK_DEV * groups
    slot_count = frames_dev * max_slots

    in_vmem = pl.BlockSpec(memory_space=pltpu.VMEM)
    row_count = frames_dev * blocks_per_device
    exact = [part.reshape(row_count, pixel_width) for part in (intensity, correction)]
    local_rows = jnp.pad(exact[0], ((0, row_count), (0, 0))) + jnp.pad(exact[1], ((row_count, 0), (0, 0)))
    local_rows = local_rows.astype(jnp.bfloat16)
    depth = slot_count * pixel_width

    split = splitting.reshape(depth, voxels)

    near, of_even, of_odd = gather_half(local_rows, exact, bricks)
    *near, block_count, pix_index, vox_offset = lax.optimization_barrier(
        (*near, block_count, pix_index, vox_offset)
    ) if len(near) == 1 else (near[0], *lax.optimization_barrier((near[1], block_count, pix_index, vox_offset)))
    far = [swap(part, bricks, 1, 1) for part in near]
    live = jnp.arange(max_slots, dtype=jnp.int32) < block_count[:, :, None]
    index = pix_index * (block_rows + 3) + jnp.where(live, vox_offset, block_rows + 2)
    meta = pl.pallas_call(
        functools.partial(
            prepare_kernel, of_even, of_odd, blocks_per_device, block_rows, bricks, groups, max_slots
        ),
        out_shape=jax.ShapeDtypeStruct((2 * CHANNELS * slot_count, pixel_width), jnp.int32),
        in_specs=[in_vmem],
        out_specs=in_vmem,
        compiler_params=pltpu.CompilerParams(vmem_limit_bytes=VMEM_LIMIT),
        name="prepare",
    )(index.reshape(frames_dev, max_slots))

    early = pl.pallas_call(
        functools.partial(pick_kernel, frames_dev, max_slots),
        out_shape=jax.ShapeDtypeStruct((CHANNELS * slot_count, pixel_width), jnp.float32),
        in_specs=[in_vmem] * (len(near) + 1),
        out_specs=in_vmem,
        compiler_params=pltpu.CompilerParams(vmem_limit_bytes=VMEM_LIMIT),
        name="pick_near",
    )(*near, meta)
    edge_rows = -(-CHANNELS * groups // 16) * 16
    inner_rows = CHANNELS * BLK_DEV * groups
    picked, *edges = pl.pallas_call(
        functools.partial(edge_kernel, frames_dev, max_slots, groups, len(far)),
        out_shape=[jax.ShapeDtypeStruct((CHANNELS * slot_count, pixel_width), jnp.float32)]
        + [jax.ShapeDtypeStruct((CHANNELS, voxels), jnp.float32)] * groups,
        in_specs=[in_vmem] * (len(far) + 3),
        out_specs=[in_vmem] * (1 + groups),
        scratch_shapes=[pltpu.VMEM((edge_rows, depth), jnp.bfloat16)],
        compiler_params=pltpu.CompilerParams(vmem_limit_bytes=VMEM_LIMIT),
        cost_estimate=pl.CostEstimate(
            flops=2 * edge_rows * depth * voxels, bytes_accessed=2 * depth * voxels, transcendentals=0
        ),
        name="edges",
    )(early, *far, meta, split)
    blocks = pl.pallas_call(
        functools.partial(inner_kernel, frames_dev, max_slots, groups),
        out_shape=[jax.ShapeDtypeStruct((CHANNELS * BLK_DEV, voxels), jnp.float32)] * groups,
        in_specs=[in_vmem] * 3,
        out_specs=[in_vmem] * groups,
        scratch_shapes=[pltpu.VMEM((inner_rows, depth), jnp.bfloat16)],
        compiler_params=pltpu.CompilerParams(vmem_limit_bytes=VMEM_LIMIT),
        cost_estimate=pl.CostEstimate(
            flops=2 * inner_rows * depth * voxels, bytes_accessed=2 * depth * voxels, transcendentals=0
        ),
        name="inner",
    )(picked, meta, split)

    def to_owner(parts):
        return [
            lax.ppermute(parts[step], "frame", [(i, (i + step) % groups) for i in range(groups)])
            for step in range(1, groups)
        ]

    arrived = to_owner(edges)
    overhang = pl.pallas_call(
        sum_kernel,
        out_shape=jax.ShapeDtypeStruct((CHANNELS, voxels), jnp.float32),
        in_specs=[in_vmem] * groups,
        out_specs=in_vmem,
        compiler_params=pltpu.CompilerParams(vmem_limit_bytes=VMEM_LIMIT),
        cost_estimate=pl.CostEstimate(flops=10**9, bytes_accessed=0, transcendentals=0),
        name="sum_edges",
    )(edges[0], *arrived)
    received = to_owner(blocks)
    turn = [(i, i) for i in range(bricks, top * bricks)]
    for i in range(bricks):
        turn.append((i, i + 1 if i + 1 < bricks else top * bricks + i))
        turn.append((top * bricks + i, top * bricks + i - 1 if i else 0))
    handed = lax.ppermute(overhang, ("frame", "brick"), turn)
    merged, weight = pl.pallas_call(
        functools.partial(finish_kernel, groups),
        out_shape=[jax.ShapeDtypeStruct((BLK_DEV, voxels), jnp.float32)] * 2,
        in_specs=[in_vmem] * (groups + 1),
        out_specs=[in_vmem] * 2,
        compiler_params=pltpu.CompilerParams(vmem_limit_bytes=VMEM_LIMIT),
        name="finish",
    )(handed, blocks[0], *received)
    return (merged[None], weight[None])


def solution(mesh):
    placed = (
        P("frame", "brick", None),
        P("frame", "brick", None),
        P("frame", "brick", None, None, None),
        P("frame", "brick"),
        P("frame", "brick", None),
        P("frame", "brick", None),
    )
    return jax.shard_map(
        on_device,
        mesh=mesh,
        in_specs=placed,
        out_specs=(P("brick", "frame", None), P("brick", "frame", None)),
        check_vma=False,
    )
```

```python
import functools

import jax
import jax.numpy as jnp
from jax import lax
from jax.experimental import pallas as pl
from jax.experimental.pallas import tpu as pltpu
from jax.sharding import PartitionSpec as P

BLK_DEV = 16
CHANNELS = 2
VMEM_LIMIT = 8 * 1024 * 1024
BLOCK_ROWS = CHANNELS * BLK_DEV + 8


def join_kernel(spare, *refs):
    refs, out_ref, at = refs[:-1], refs[-1], 0
    for ref in refs if spare is None else refs[:-1]:
        out_ref[pl.ds(at, ref.shape[0])] = ref[...]
        at += ref.shape[0]
    if spare is not None:
        own = refs[-1]

        @pl.when(lax.axis_index("brick") % 2 == 0)
        def _():
            out_ref[pl.ds(spare * own.shape[0], own.shape[0])] = own[...]


def join(parts, spare=None):
    in_vmem = pl.BlockSpec(memory_space=pltpu.VMEM)
    count = sum(part.shape[0] for part in (parts if spare is None else parts[:-1]))
    return pl.pallas_call(
        functools.partial(join_kernel, spare),
        out_shape=jax.ShapeDtypeStruct((count,) + parts[0].shape[1:], parts[0].dtype),
        in_specs=[in_vmem] * len(parts),
        out_specs=in_vmem,
        compiler_params=pltpu.CompilerParams(vmem_limit_bytes=VMEM_LIMIT),
        cost_estimate=pl.CostEstimate(flops=10**11, bytes_accessed=0, transcendentals=0),
        name="join_rows",
    )(*parts)


def swap(rows, bricks, even, odd):
    return lax.ppermute(rows, "brick", [(i, i ^ (odd if i % 2 else even)) for i in range(bricks)])


def pair_kernel(own_ref, *refs):
    refs, out_ref = refs[:-1], refs[-1]
    out_ref[0] = own_ref[...]
    for at, ref in enumerate(refs):
        out_ref[1, pl.ds(at * ref.shape[0], ref.shape[0]), :] = ref[...].astype(jnp.bfloat16)


def pair_up(own, others):
    in_vmem = pl.BlockSpec(memory_space=pltpu.VMEM)
    return pl.pallas_call(
        pair_kernel,
        out_shape=jax.ShapeDtypeStruct((2,) + own.shape, own.dtype),
        in_specs=[in_vmem] * (1 + len(others)),
        out_specs=in_vmem,
        compiler_params=pltpu.CompilerParams(vmem_limit_bytes=VMEM_LIMIT),
        name="pair_rows",
    )(own, *others)


def gather_half(rows, exact, bricks):
    held = rows[None]
    if bricks == 16:
        held = pair_up(rows, [swap(part, bricks, 1, 1) for part in exact])
        even, odd, spare = (4, 2, 4), (8, 14, 12), 2
        arrived = {at: swap(held, bricks, even[at], odd[at]) for at in (0, 1, 2)}
        arrived = [arrived[at] for at in range(len(even))]
        handed = swap(arrived[0], bricks, 2, 2)
        even, odd = even + (even[0] ^ 2,), odd + (odd[0] ^ 2,)
        of_even = [d ^ c for at, d in enumerate(even) for d in (0 if at == spare else d,) for c in (0, 1)]
        of_odd = [d ^ c for d in odd for c in (0, 1)]
        of_even, of_odd = of_even + [d ^ 1 for d in of_odd], of_odd + [d ^ 1 for d in of_even]
        return [join(arrived[:2]), join([arrived[2], handed, held], 0)], of_even, of_odd
    parts, distances, step = [held], [0], bricks // 2
    while step > 1:
        arrived = swap(jnp.concatenate(parts, axis=0), bricks, step, step)
        parts, distances = parts + [arrived], distances + [d ^ step for d in distances]
        step //= 2
    distances = distances + [d ^ 1 for d in distances]
    return [join(parts)], distances, distances


def place_of(distance, distances):
    place = 0
    for at, d in enumerate(distances):
        place = place + jnp.where(distance == d, at, 0)
    return place


def prepare_kernel(of_even, of_odd, per_owner, block_rows, bricks, groups, slots, index_ref, meta_ref):
    brick, group = lax.axis_index("brick"), lax.axis_index("frame")
    frames = index_ref.shape[0]
    pair = slots * CHANNELS
    wide = (pair, meta_ref.shape[1])
    row = lax.broadcasted_iota(jnp.int32, wide, 0)
    channel = row % CHANNELS
    mine = lax.broadcasted_iota(jnp.int32, (pair, slots), 1) == (
        lax.broadcasted_iota(jnp.int32, (pair, slots), 0) // CHANNELS
    )
    for frame in range(frames):
        line = jnp.broadcast_to(index_ref[pl.ds(frame, 1), :], mine.shape)
        index = jnp.broadcast_to(jnp.sum(jnp.where(mine, line, 0), axis=1, keepdims=True), wide)
        pixel_block = index // (block_rows + 3)
        offset = index - pixel_block * (block_rows + 3)
        owner = pixel_block // per_owner
        place = jnp.where(brick % 2 == 0, place_of(owner ^ brick, of_even), place_of(owner ^ brick, of_odd))
        target = (place * CHANNELS + channel) * per_owner + (pixel_block - owner * per_owner)
        meta_ref[pl.ds(frame * pair, pair), :] = target
        low, high = offset == 0, offset == block_rows + 1
        holder = jnp.where(low, groups - 1, jnp.where(high, 0, (offset - 1) // BLK_DEV))
        step = holder - group
        step = jnp.where(step < 0, step + groups, step)
        inside = offset - 1 - holder * BLK_DEV + BLK_DEV * channel
        goal = step * BLOCK_ROWS + jnp.where(low | high, CHANNELS * BLK_DEV + channel, inside)
        live = offset < block_rows + 2
        live = live & ~(low & (brick == 0)) & ~(high & (brick == bricks - 1))
        meta_ref[pl.ds((frames + frame) * pair, pair), :] = jnp.where(live, goal, -1)


def pick(frames, slots, frame, start, rows_ref, meta_ref):
    count, per_brick, pixels = rows_ref.shape
    per_owner = per_brick // (CHANNELS * frames)
    reach = count * CHANNELS * per_owner
    pair = CHANNELS * slots
    lane = lax.broadcasted_iota(jnp.int32, (pair, pixels), 1) + start * CHANNELS * per_owner
    target = meta_ref[pl.ds(frame * pair, pair), :]
    chosen = jnp.concatenate(
        [(target == lane + at).astype(jnp.float32) for at in range(0, reach, pixels)], axis=1
    ).astype(jnp.bfloat16)
    own = jnp.concatenate(
        [rows_ref[:, pl.ds((c * frames + frame) * per_owner, per_owner), :] for c in range(CHANNELS)], axis=1
    )
    return jnp.dot(chosen, own.reshape(reach, pixels), preferred_element_type=jnp.float32)


def pick_all(frames, slots, frame, start, refs, meta_ref):
    total = 0.0
    for ref in refs:
        total = total + pick(frames, slots, frame, start, ref, meta_ref)
        start += ref.shape[0]
    return total


def pick_kernel(frames, slots, *refs):
    near, (meta_ref, picked_ref) = refs[:-2], refs[-2:]
    pair = CHANNELS * slots
    for frame in range(frames):
        picked_ref[pl.ds(frame * pair, pair), :] = pick_all(frames, slots, frame, 0, near, meta_ref)


def edge_kernel(frames, slots, groups, count, early_ref, *refs):
    far, (meta_ref, split_ref), refs = refs[:count], refs[count : count + 2], refs[count + 2 :]
    picked_ref, edges, placed_ref = refs[0], refs[1 : 1 + groups], refs[1 + groups]
    half, pixels = sum(ref.shape[0] for ref in far), far[0].shape[2]
    pair = CHANNELS * slots
    row = lax.broadcasted_iota(jnp.int32, (placed_ref.shape[0], pixels), 0)
    row = row // CHANNELS * BLOCK_ROWS + CHANNELS * BLK_DEV + row % CHANNELS
    for frame in range(frames):
        picked = early_ref[pl.ds(frame * pair, pair), :]
        picked = picked + pick_all(frames, slots, frame, half, far, meta_ref)
        picked_ref[pl.ds(frame * pair, pair), :] = picked
        goal = meta_ref[pl.ds((frames + frame) * pair, pair), :]
        for slot in range(slots):
            laid = jnp.zeros(row.shape, jnp.float32)
            for c in range(CHANNELS):
                at = CHANNELS * slot + c
                value = jnp.broadcast_to(picked[at : at + 1], row.shape)
                laid = jnp.where(row == jnp.broadcast_to(goal[at : at + 1], row.shape), value, laid)
            place = (frame * slots + slot) * pixels
            placed_ref[:, pl.ds(place, pixels)] = laid.astype(jnp.bfloat16)
    total = jnp.dot(placed_ref[...], split_ref[...], preferred_element_type=jnp.float32)
    for block in range(groups):
        edges[block][...] = total[CHANNELS * block : CHANNELS * (block + 1)]


def inner_kernel(frames, slots, groups, picked_ref, meta_ref, split_ref, *refs):
    inner, placed_ref = refs[:groups], refs[groups]
    pixels = picked_ref.shape[1]
    pair = CHANNELS * slots
    row = lax.broadcasted_iota(jnp.int32, (BLK_DEV, pixels), 0)
    zero = jnp.zeros(row.shape, jnp.float32)
    for frame in range(frames):
        picked = picked_ref[pl.ds(frame * pair, pair), :]
        goal = meta_ref[pl.ds((frames + frame) * pair, pair), :]
        for slot in range(slots):
            parts = []
            for block in range(groups):
                for c in range(CHANNELS):
                    at = CHANNELS * slot + c
                    value = jnp.broadcast_to(picked[at : at + 1], row.shape)
                    here = jnp.broadcast_to(goal[at : at + 1], row.shape) - (block * BLOCK_ROWS + c * BLK_DEV)
                    parts.append(jnp.where(row == here, value, zero))
            place = (frame * slots + slot) * pixels
            placed_ref[:, pl.ds(place, pixels)] = jnp.concatenate(parts, axis=0).astype(jnp.bfloat16)
    total = jnp.dot(placed_ref[...], split_ref[...], preferred_element_type=jnp.float32)
    for block in range(groups):
        base = block * CHANNELS * BLK_DEV
        inner[block][...] = total[base : base + CHANNELS * BLK_DEV]


def sum_kernel(*refs):
    total = refs[0][...]
    for ref in refs[1:-1]:
        total = total + ref[...]
    refs[-1][...] = total


def finish_kernel(groups, handed_ref, *refs):
    parts, (merged_ref, weight_ref) = refs[:groups], refs[groups:]
    group = lax.axis_index("frame")
    row = jnp.where(group == 0, 0, jnp.where(group == groups - 1, BLK_DEV - 1, -1))
    here = lax.broadcasted_iota(jnp.int32, merged_ref.shape, 0) == row
    totals = []
    for c in range(CHANNELS):
        rows = pl.ds(c * BLK_DEV, BLK_DEV)
        total = jnp.where(here, handed_ref[pl.ds(c, 1), :], 0.0)
        for part in parts:
            total = total + part[rows, :]
        totals.append(total)
    weight_ref[...] = totals[1]
    merged_ref[...] = totals[0] / jnp.maximum(totals[1], 1.0)


def on_device(intensity, correction, splitting, block_count, pix_index, vox_offset):
    frames_dev, blocks_per_device, pixel_width = intensity.shape
    max_slots = splitting.shape[2]
    voxels = splitting.shape[4]
    bricks = lax.axis_size("brick")
    groups = lax.axis_size("frame")
    top = groups - 1
    block_rows = BLK_DEV * groups
    slot_count = frames_dev * max_slots

    in_vmem = pl.BlockSpec(memory_space=pltpu.VMEM)
    row_count = frames_dev * blocks_per_device
    exact = [part.reshape(row_count, pixel_width) for part in (intensity, correction)]
    local_rows = jnp.pad(exact[0], ((0, row_count), (0, 0))) + jnp.pad(exact[1], ((row_count, 0), (0, 0)))
    local_rows = local_rows.astype(jnp.bfloat16)
    depth = slot_count * pixel_width

    split = splitting.reshape(depth, voxels)

    near, of_even, of_odd = gather_half(local_rows, exact, bricks)
    *near, block_count, pix_index, vox_offset = lax.optimization_barrier(
        (*near, block_count, pix_index, vox_offset)
    ) if len(near) == 1 else (near[0], *lax.optimization_barrier((near[1], block_count, pix_index, vox_offset)))
    far = [swap(part, bricks, 1, 1) for part in near]
    live = jnp.arange(max_slots, dtype=jnp.int32) < block_count[:, :, None]
    index = pix_index * (block_rows + 3) + jnp.where(live, vox_offset, block_rows + 2)
    meta = pl.pallas_call(
        functools.partial(
            prepare_kernel, of_even, of_odd, blocks_per_device, block_rows, bricks, groups, max_slots
        ),
        out_shape=jax.ShapeDtypeStruct((2 * CHANNELS * slot_count, pixel_width), jnp.int32),
        in_specs=[in_vmem],
        out_specs=in_vmem,
        compiler_params=pltpu.CompilerParams(vmem_limit_bytes=VMEM_LIMIT),
        name="prepare",
    )(index.reshape(frames_dev, max_slots))

    early = pl.pallas_call(
        functools.partial(pick_kernel, frames_dev, max_slots),
        out_shape=jax.ShapeDtypeStruct((CHANNELS * slot_count, pixel_width), jnp.float32),
        in_specs=[in_vmem] * (len(near) + 1),
        out_specs=in_vmem,
        compiler_params=pltpu.CompilerParams(vmem_limit_bytes=VMEM_LIMIT),
        name="pick_near",
    )(*near, meta)
    edge_rows = -(-CHANNELS * groups // 16) * 16
    inner_rows = CHANNELS * BLK_DEV * groups
    picked, *edges = pl.pallas_call(
        functools.partial(edge_kernel, frames_dev, max_slots, groups, len(far)),
        out_shape=[jax.ShapeDtypeStruct((CHANNELS * slot_count, pixel_width), jnp.float32)]
        + [jax.ShapeDtypeStruct((CHANNELS, voxels), jnp.float32)] * groups,
        in_specs=[in_vmem] * (len(far) + 3),
        out_specs=[in_vmem] * (1 + groups),
        scratch_shapes=[pltpu.VMEM((edge_rows, depth), jnp.bfloat16)],
        compiler_params=pltpu.CompilerParams(vmem_limit_bytes=VMEM_LIMIT),
        cost_estimate=pl.CostEstimate(
            flops=2 * edge_rows * depth * voxels, bytes_accessed=2 * depth * voxels, transcendentals=0
        ),
        name="edges",
    )(early, *far, meta, split)
    blocks = pl.pallas_call(
        functools.partial(inner_kernel, frames_dev, max_slots, groups),
        out_shape=[jax.ShapeDtypeStruct((CHANNELS * BLK_DEV, voxels), jnp.float32)] * groups,
        in_specs=[in_vmem] * 3,
        out_specs=[in_vmem] * groups,
        scratch_shapes=[pltpu.VMEM((inner_rows, depth), jnp.bfloat16)],
        compiler_params=pltpu.CompilerParams(vmem_limit_bytes=VMEM_LIMIT),
        cost_estimate=pl.CostEstimate(
            flops=2 * inner_rows * depth * voxels, bytes_accessed=2 * depth * voxels, transcendentals=0
        ),
        name="inner",
    )(picked, meta, split)

    def to_owner(parts):
        return [
            lax.ppermute(parts[step], "frame", [(i, (i + step) % groups) for i in range(groups)])
            for step in range(1, groups)
        ]

    arrived = to_owner(edges)
    overhang = pl.pallas_call(
        sum_kernel,
        out_shape=jax.ShapeDtypeStruct((CHANNELS, voxels), jnp.float32),
        in_specs=[in_vmem] * groups,
        out_specs=in_vmem,
        compiler_params=pltpu.CompilerParams(vmem_limit_bytes=VMEM_LIMIT),
        cost_estimate=pl.CostEstimate(flops=10**9, bytes_accessed=0, transcendentals=0),
        name="sum_edges",
    )(edges[0], *arrived)
    received = to_owner(blocks)
    turn = [(i, i) for i in range(bricks, top * bricks)]
    for i in range(bricks):
        turn.append((i, i + 1 if i + 1 < bricks else top * bricks + i))
        turn.append((top * bricks + i, top * bricks + i - 1 if i else 0))
    handed = lax.ppermute(overhang, ("frame", "brick"), turn)
    merged, weight = pl.pallas_call(
        functools.partial(finish_kernel, groups),
        out_shape=[jax.ShapeDtypeStruct((BLK_DEV, voxels), jnp.float32)] * 2,
        in_specs=[in_vmem] * (groups + 1),
        out_specs=[in_vmem] * 2,
        compiler_params=pltpu.CompilerParams(vmem_limit_bytes=VMEM_LIMIT),
        name="finish",
    )(handed, blocks[0], *received)
    return (merged[None], weight[None])


def solution(mesh):
    placed = (
        P("frame", "brick", None),
        P("frame", "brick", None),
        P("frame", "brick", None, None, None),
        P("frame", "brick"),
        P("frame", "brick", None),
        P("frame", "brick", None),
    )
    return jax.shard_map(
        on_device,
        mesh=mesh,
        in_specs=placed,
        out_specs=(P("brick", "frame", None), P("brick", "frame", None)),
        check_vma=False,
    )
```
